32 devices in a mesh: face: 16 (over z, y, core), depth: 2 (over x).
Axes of the slice: x: 2, y: 2, z: 4, core: 2. Of those that a mesh axis runs over, the one named last changes fastest.
Arguments:
- thermal_field: float32 [2, 16, 2, 2048], P(None, 'face', 'depth'), may hold values from -6 to 6
- lumped_storage: float32 [2, 16, 2, 2048], P(None, 'face', 'depth'), may hold values from 1 to 4
- simplex_vertices: int32 [2, 16, 2, 4, 8192], P(None, 'face', 'depth'), may hold values from 0 to 2047
- stiffness_entries: float32 [2, 16, 2, 10, 8192], P(None, 'face', 'depth'), may hold values from -0.3 to 2, as said below
- interface_vertices: int32 [2, 16, 2, 2, 256], P(None, 'face', 'depth'), may hold values from 0 to 2047, as said below
- touching_triangle_vertices: int32 [2, 16, 3, 1024], P(None, 'face'), may hold values from 0 to 2047
- partner_lookup: int32 [16, 1024], replicated, may hold values from 0 to 16383, as said below
- engaged_flags: int32 [16, 1024], P('face'), may hold values 0 or 1
- rotor_gap_quantities: float32 [3, 16, 1024], P(None, 'face'), may hold values from -6 to 6
- lining_orthogonal_motion: float32 [16, 1024], P('face'), may hold values from -6 to 6
- touching_transfer_factor: float32 [16, 1024], P('face'), may hold values from 2 to 16
Outputs:
- advanced_thermal_field: float32 [2, 16, 2, 2048], P(None, 'face', 'depth')
- pressure: float32 [16, 1024], P('face')
The draws below stay inside these ranges and needn't reach their ends.
Inputs may be any that keep to these rules, and one draw needn't show every extreme that they name: `stiffness_entries`: diagonal entries (the first four components) lie in [1, 2], off-diagonal ones in [-0.3, -0.05]. `interface_vertices`: the two lists of one body on one device name 512 different nodes. Position i of a block's upper list and position i of the lower list of the block above are copies of one node. `partner_lookup`: A disc face may meet a pad face of any patch; several disc faces may meet one pad face.
All inputs are finite; a program needn't handle non-finite values. No bound on the sum of `engaged_flags` on one device may be relied on, other than what follows from the above.
Results may differ from the reference program's by a relative error of at most 0.00002.
Values sent between devices are 32-bit elements; how exact they have to be, the bound alone decides.
A program may use at most 64 MiB of HBM per device.

```python
import math
import jax
import jax.numpy as jnp
from jax import lax

TET_DEV = 8192
CF = 1024
MESH_POINTS_LOCAL = 2048
IFACE = 256
BOUNDARY_TILES = 16
LAYER_TIERS = 2


def draw_stiffness_entries(key, part):
    array_shape = (2, BOUNDARY_TILES, LAYER_TIERS, 10, TET_DEV)
    base = jax.random.uniform(key, array_shape, jnp.float32)
    component = lax.broadcasted_iota(jnp.int32, array_shape, 3)
    return jnp.where(component < 4, 1.0 + base, -0.05 - 0.25 * base)


def draw_interface_vertices(key, part):
    total = 2 * BOUNDARY_TILES * LAYER_TIERS
    keys = jax.random.split(jax.random.fold_in(key, 17), total)
    orders = jax.vmap(lambda single: jax.random.permutation(single, MESH_POINTS_LOCAL))(keys)
    picked = orders[:, :2 * IFACE].astype(jnp.int32)
    return picked.reshape(2, BOUNDARY_TILES, LAYER_TIERS, 2, IFACE)


def draw_partner_lookup(key, part):
    patch_key, face_key = jax.random.split(jax.random.fold_in(key, 29))
    grid_shape = (BOUNDARY_TILES, CF)
    own_patch = lax.broadcasted_iota(jnp.int32, grid_shape, 0)
    slot = lax.broadcasted_iota(jnp.int32, grid_shape, 1)
    far_patch = jax.random.randint(patch_key, grid_shape, 0, BOUNDARY_TILES, jnp.int32)
    within = jax.random.randint(face_key, grid_shape, 0, CF, jnp.int32)
    far_patch = jnp.where(slot == 0, jnp.mod(own_patch + BOUNDARY_TILES // 2, BOUNDARY_TILES), far_patch)
    within = jnp.where(slot == 0, CF - 1, within)
    far_patch = jnp.where(slot == 1, jnp.mod(own_patch + 1, BOUNDARY_TILES), far_patch)
    within = jnp.where(slot == 1, 0, within)
    return (far_patch * CF + within).astype(jnp.int32)


def touch_ends(array, own_key, low, top_value):
    extent = array.shape
    spot = [jax.random.randint(jax.random.fold_in(own_key, axis), (), 0, extent[axis]) for axis in range(len(extent))]
    array = array.at[tuple(spot)].set(low)
    longest = extent.index(max(extent))
    spot[longest] = (spot[longest] + 1) % extent[longest]
    return array.at[tuple(spot)].set(top_value)


def levels(key, extent, cuts, low, largest):
    def one(axis_at, blocks):
        draws = jax.random.uniform(jax.random.fold_in(jax.random.fold_in(key, 6), axis_at), (blocks,), jnp.float32, low / len(cuts), largest / len(cuts))
        return jnp.repeat(jnp.exp(draws), extent[axis_at] // blocks).reshape((-1,) + (1,) * (len(extent) - axis_at - 1))

    factor_of = one(*cuts[0])
    for cut in cuts[1:]:
        factor_of = factor_of * one(*cut)
    return factor_of


def gaussian(own_key, extent, width, limit, cuts=(), kind=jnp.bfloat16):
    factor_of = levels(own_key, extent, cuts, -0.22, 0.18) if cuts else 1.0
    values = jax.random.normal(own_key, extent, jnp.float32) * width * factor_of
    return jnp.minimum(jnp.maximum(values, -limit), limit).astype(kind)


def setup_inputs(seed: int = 0) -> dict:
    seeds = jax.random.split(jax.random.key(seed), 12)
    thermal_field = gaussian(seeds[0], (2, BOUNDARY_TILES, LAYER_TIERS, MESH_POINTS_LOCAL), 1.0, 6.0, ((1, 16), (2, 2)), jnp.float32)
    lumped_storage = jnp.clip(jnp.exp(math.log(4.0) - 1.3862944 * jax.random.uniform(seeds[1], (2, BOUNDARY_TILES, LAYER_TIERS, MESH_POINTS_LOCAL), jnp.float32) ** levels(seeds[1], (2, BOUNDARY_TILES, LAYER_TIERS, MESH_POINTS_LOCAL), ((1, 16), (2, 2)), -0.2, 0.2)), 1.0, 4.0)
    simplex_vertices = touch_ends(jax.random.randint(seeds[2], (2, BOUNDARY_TILES, LAYER_TIERS, 4, TET_DEV), 0, MESH_POINTS_LOCAL), jax.random.fold_in(seeds[2], 1), 0, MESH_POINTS_LOCAL - 1).astype(jnp.int32)
    stiffness_entries = draw_stiffness_entries(jax.random.fold_in(seeds[11], 71), 0)
    interface_vertices = draw_interface_vertices(jax.random.fold_in(seeds[11], 71), 0)
    touching_triangle_vertices = touch_ends(jax.random.randint(seeds[5], (2, BOUNDARY_TILES, 3, CF), 0, MESH_POINTS_LOCAL), jax.random.fold_in(seeds[5], 1), 0, MESH_POINTS_LOCAL - 1).astype(jnp.int32)
    partner_lookup = draw_partner_lookup(jax.random.fold_in(seeds[11], 71), 0)
    engaged_flags = touch_ends((jax.random.randint(seeds[7], (BOUNDARY_TILES, CF), 0, 4) < 3).astype(jnp.int32), jax.random.fold_in(seeds[7], 1), 0, 1)
    rotor_gap_quantities = gaussian(seeds[8], (3, BOUNDARY_TILES, CF), 1.0, 6.0, ((1, 16),), jnp.float32)
    lining_orthogonal_motion = gaussian(seeds[9], (BOUNDARY_TILES, CF), 1.0, 6.0, ((0, 16),), jnp.float32)
    touching_transfer_factor = jnp.clip(jnp.exp(math.log(16.0) - 2.0794415 * jax.random.uniform(seeds[10], (BOUNDARY_TILES, CF), jnp.float32) ** levels(seeds[10], (BOUNDARY_TILES, CF), ((0, 16),), -0.2, 0.2)), 2.0, 16.0)
    return {"thermal_field": thermal_field, "lumped_storage": lumped_storage, "simplex_vertices": simplex_vertices, "stiffness_entries": stiffness_entries, "interface_vertices": interface_vertices, "touching_triangle_vertices": touching_triangle_vertices, "partner_lookup": partner_lookup, "engaged_flags": engaged_flags, "rotor_gap_quantities": rotor_gap_quantities, "lining_orthogonal_motion": lining_orthogonal_motion, "touching_transfer_factor": touching_transfer_factor}


increment_factor = 0.05
nitsche = 1.0
film_floor = 0.25


def element_residual(values, corners, entries):
    picked = values[corners]
    row_one = entries[0] * picked[0] + entries[4] * picked[1] + entries[5] * picked[2] + entries[6] * picked[3]
    row_two = entries[4] * picked[0] + entries[1] * picked[1] + entries[7] * picked[2] + entries[8] * picked[3]
    row_three = entries[5] * picked[0] + entries[7] * picked[1] + entries[2] * picked[2] + entries[9] * picked[3]
    row_four = entries[6] * picked[0] + entries[8] * picked[1] + entries[9] * picked[2] + entries[3] * picked[3]
    stacked = -jnp.stack([row_one, row_two, row_three, row_four])
    return jax.ops.segment_sum(stacked.reshape(-1), corners.reshape(-1), num_segments=values.shape[0])


def touching_triangle_values(values, corners):
    picked = values[corners]
    return (picked[0] + picked[1] + picked[2]) / 3.0


def spread_faces(face_rates, corners, solid_vertex_total):
    shares = jnp.broadcast_to(face_rates / 3.0, corners.shape)
    return jax.ops.segment_sum(shares.reshape(-1), corners.reshape(-1), num_segments=solid_vertex_total)


def set_rims(values, low_at, up_at, low_set, up_set):
    return values.at[low_at].set(low_set).at[up_at].set(up_set)


def reference(thermal_field, lumped_storage, simplex_vertices, stiffness_entries, interface_vertices, touching_triangle_vertices, partner_lookup, engaged_flags, rotor_gap_quantities, lining_orthogonal_motion, touching_transfer_factor):
    solid_vertex_total = thermal_field.shape[-1]
    simplex_total = simplex_vertices.shape[-1]
    cell_share = lax.map(lambda blocks: element_residual(blocks[0], blocks[1], blocks[2]),
                           (thermal_field.reshape(-1, solid_vertex_total), simplex_vertices.reshape(-1, 4, simplex_total), stiffness_entries.reshape(-1, 10, simplex_total)))
    thermal_imbalance = cell_share.reshape(thermal_field.shape)
    boundary_restrictions = jax.vmap(jax.vmap(touching_triangle_values))(thermal_field[:, :, 0, :], touching_triangle_vertices)
    flat_match = partner_lookup.reshape(-1)
    active_mask = engaged_flags.astype(jnp.float32)
    pad_normals = lining_orthogonal_motion.reshape(-1)[flat_match].reshape(partner_lookup.shape)
    pad_traces = boundary_restrictions[1].reshape(-1)[flat_match].reshape(partner_lookup.shape)
    pressure = active_mask * jnp.maximum(rotor_gap_quantities[2] + nitsche * (rotor_gap_quantities[0] - pad_normals - rotor_gap_quantities[1]), 0.0)
    disc_rate = active_mask * touching_transfer_factor * (film_floor + pressure) * (pad_traces - boundary_restrictions[0])
    pad_rate = -jax.ops.segment_sum(disc_rate.reshape(-1), flat_match, num_segments=flat_match.shape[0]).reshape(partner_lookup.shape)
    face_rates = jnp.stack([disc_rate, pad_rate])
    nodal = jax.vmap(jax.vmap(lambda rates_row, corners: spread_faces(rates_row, corners, solid_vertex_total)))(face_rates, touching_triangle_vertices)
    thermal_imbalance = thermal_imbalance.at[:, :, 0, :].add(nodal)
    lower = interface_vertices[:, :, :, 0, :]
    upper = interface_vertices[:, :, :, 1, :]
    low_values = jnp.take_along_axis(thermal_imbalance, lower, axis=3)
    up_values = jnp.take_along_axis(thermal_imbalance, upper, axis=3)
    zeros_row = jnp.zeros_like(low_values[:, :, :1])
    from_below = jnp.concatenate([zeros_row, up_values[:, :, :-1]], axis=2)
    from_above = jnp.concatenate([low_values[:, :, 1:], zeros_row], axis=2)
    low_new = low_values + from_below
    up_new = up_values + from_above
    rim_count = lower.shape[-1]
    gathered_imbalance = jax.vmap(set_rims)(thermal_imbalance.reshape(-1, solid_vertex_total), lower.reshape(-1, rim_count), upper.reshape(-1, rim_count),
                                   low_new.reshape(-1, rim_count), up_new.reshape(-1, rim_count)).reshape(thermal_imbalance.shape)
    advanced_thermal_field = thermal_field + increment_factor * gathered_imbalance / lumped_storage
    return advanced_thermal_field, pressure
```

```python
import functools

import jax
import jax.numpy as jnp
from jax import lax
from jax.experimental import pallas as pl
from jax.experimental.pallas import tpu as pltpu
from jax.sharding import PartitionSpec as P

increment_factor = 0.05
nitsche = 1.0
film_floor = 0.25

LANES = 128
SUB = 8
MESH = pl.DeviceIdType.MESH


def row_spread(row, count):
    return jnp.broadcast_to(row, (count, LANES))


def pick(row_of, rows, index):
    low = jnp.bitwise_and(index, LANES - 1)
    high = jnp.right_shift(index, 7)
    out = jnp.zeros(index.shape, jnp.float32)
    for r in range(rows):
        got = jnp.take_along_axis(row_of(r), low, axis=1, mode="promise_in_bounds")
        out = jnp.where(high == r, got, out)
    return out


def split(value, pieces):
    parts = []
    for _ in range(pieces - 1):
        head = value.astype(jnp.bfloat16).astype(jnp.float32)
        parts.append(head)
        value = value - head
    parts.append(value)
    return parts


def add_into(indices, values, rows, pieces):
    lane_iota = lax.broadcasted_iota(jnp.int32, (LANES, LANES), 0).astype(jnp.float32).astype(jnp.bfloat16)
    row_iota = lax.broadcasted_iota(jnp.int32, (rows, LANES), 0).astype(jnp.float32).astype(jnp.bfloat16)
    one = jnp.ones((LANES, LANES), jnp.bfloat16)
    zero = jnp.zeros((LANES, LANES), jnp.bfloat16)
    zero_rows = jnp.zeros((rows, LANES), jnp.bfloat16)
    left = [[] for _ in range(pieces)]
    right = []
    for index, value in zip(indices, values):
        low = jnp.bitwise_and(index, LANES - 1).astype(jnp.float32)
        high = jnp.right_shift(index, 7).astype(jnp.float32)
        parts = split(value, pieces)

        def wide(array, s, count):
            base = row_spread(array[s : s + 1, :], 16).astype(jnp.bfloat16)
            return jnp.concatenate([base] * (count // 16), axis=0) if count > 16 else base

        for s in range(SUB):
            right.append(jnp.where(lane_iota == wide(low, s, LANES), one, zero))
            hit = row_iota == wide(high, s, rows)
            for k in range(pieces):
                left[k].append(jnp.where(hit, wide(parts[k], s, rows), zero_rows))
    left = jnp.concatenate([jnp.concatenate(one_piece, axis=1) for one_piece in left], axis=0)
    right = jnp.concatenate(right, axis=1)
    both = lax.dot_general(left, right, (((1,), (1,)), ((), ())), preferred_element_type=jnp.float32)
    total = both[:rows]
    for k in range(1, pieces):
        total = total + both[k * rows : (k + 1) * rows]
    return total


def spread_table(field_ref, table, body, rows):
    for r in range(rows):
        table[body, r] = row_spread(field_ref[body, r : r + 1, :], SUB)


def element_part(body, table, corners_ref, entries_ref, rows):
    chunks = entries_ref.shape[2] // SUB

    def step(j, total):
        first = pl.multiple_of(j * (4 * SUB), 4 * SUB)
        tile = pl.multiple_of(j * SUB, SUB)
        index = [corners_ref[body, pl.ds(first + c, SUB, stride=4), :] for c in range(4)]
        t = [pick(lambda r: table[body, r], rows, index[c]) for c in range(4)]
        k = [entries_ref[body, m, pl.ds(tile, SUB), :] for m in range(10)]
        out = [
            -(k[0] * t[0] + k[4] * t[1] + k[5] * t[2] + k[6] * t[3]),
            -(k[4] * t[0] + k[1] * t[1] + k[7] * t[2] + k[8] * t[3]),
            -(k[5] * t[0] + k[7] * t[1] + k[2] * t[2] + k[9] * t[3]),
            -(k[6] * t[0] + k[8] * t[1] + k[9] * t[2] + k[3] * t[3]),
        ]
        return total + add_into(index, out, rows, 2)

    return lax.fori_loop(0, chunks, step, jnp.zeros((rows, LANES), jnp.float32))


def element_kernel(field_ref, corners_ref, entries_ref, out_ref, table):
    rows = field_ref.shape[1]
    for body in range(2):
        spread_table(field_ref, table, body, rows)
        out_ref[body] = element_part(body, table, corners_ref, entries_ref, rows)


def contact_kernel(
    faces,
    layers,
    field_ref,
    storage_ref,
    part_ref,
    rim_ref,
    tri_ref,
    match_ref,
    flag_ref,
    gap_ref,
    motion_ref,
    factor_ref,
    out_ref,
    pressure_ref,
    table,
    residual,
    pad,
    spread,
    landed,
    rim_out,
    rim_in,
    pad_send,
    pad_recv,
    rate_send,
    rate_recv,
    rim_send,
    rim_recv,
):
    rows = field_ref.shape[1]
    me = lax.axis_index("face")
    layer = lax.axis_index("depth")

    barrier = pltpu.get_barrier_semaphore()

    def greet(k, carry):
        peer = lax.rem(me + k, faces)
        pl.semaphore_signal(barrier, inc=1, device_id=(peer, layer), device_id_type=MESH)
        return carry

    lax.fori_loop(1, faces, greet, 0)

    @pl.when(layer > 0)
    def _():
        pl.semaphore_signal(barrier, inc=1, device_id=(me, layer - 1), device_id_type=MESH)

    @pl.when(layer < layers - 1)
    def _():
        pl.semaphore_signal(barrier, inc=1, device_id=(me, layer + 1), device_id_type=MESH)

    traces = []
    for body in range(2):
        spread_table(field_ref, table, body, rows)
        t = [pick(lambda r: table[body, r], rows, tri_ref[body, c]) for c in range(3)]
        traces.append((t[0] + t[1] + t[2]) / 3.0)
    pad[me, 0] = motion_ref[...]
    pad[me, 1] = traces[1]

    around = (layer > 0).astype(jnp.int32) + (layer < layers - 1).astype(jnp.int32)
    pl.semaphore_wait(barrier, faces - 1 + around)

    def pad_copy(slot, peer):
        return pltpu.make_async_remote_copy(
            src_ref=pad.at[slot],
            dst_ref=pad.at[slot],
            send_sem=pad_send.at[peer],
            recv_sem=pad_recv.at[slot],
            device_id=(peer, layer),
            device_id_type=MESH,
        )

    def send_pad(k, carry):
        pad_copy(me, lax.rem(me + k, faces)).start()
        return carry

    lax.fori_loop(1, faces, send_pad, 0)

    def wait_pad(k, carry):
        peer = lax.rem(me + k, faces)
        pad_copy(peer, peer).wait_recv()
        return carry

    lax.fori_loop(1, faces, wait_pad, 0)

    line = lax.broadcasted_iota(jnp.int32, (SUB, LANES), 0)
    band = pl.multiple_of(me // SUB * SUB, SUB)
    mine = line == lax.rem(me, SUB)
    match = jnp.concatenate(
        [
            jnp.sum(
                jnp.where(mine, match_ref[pl.ds(band, SUB), s * LANES : (s + 1) * LANES], 0),
                axis=0,
                keepdims=True,
            )
            for s in range(SUB)
        ],
        axis=0,
    )
    low = jnp.bitwise_and(match, LANES - 1)
    high = jnp.right_shift(match, 7)

    def look(patch, carry):
        normal, trace = carry
        for s in range(SUB):
            hit = high == patch * SUB + s
            for_normal = row_spread(pad[patch, 0, s : s + 1, :], SUB)
            for_trace = row_spread(pad[patch, 1, s : s + 1, :], SUB)
            normal = jnp.where(
                hit, jnp.take_along_axis(for_normal, low, axis=1, mode="promise_in_bounds"), normal
            )
            trace = jnp.where(
                hit, jnp.take_along_axis(for_trace, low, axis=1, mode="promise_in_bounds"), trace
            )
        return normal, trace

    zeros = jnp.zeros((SUB, LANES), jnp.float32)
    normal, trace = lax.fori_loop(0, faces, look, (zeros, zeros))
    active = flag_ref[...].astype(jnp.float32)
    pressure = active * jnp.maximum(gap_ref[2] + nitsche * (gap_ref[0] - normal - gap_ref[1]), 0.0)
    pressure_ref[...] = pressure
    disc_rate = active * factor_ref[...] * (film_floor + pressure) * (trace - traces[0])
    spread[...] = add_into([match], [disc_rate], faces * SUB, 3)

    def rate_copy(slot, peer):
        return pltpu.make_async_remote_copy(
            src_ref=spread.at[pl.ds(pl.multiple_of(peer * SUB, SUB), SUB)],
            dst_ref=landed.at[slot],
            send_sem=rate_send.at[peer],
            recv_sem=rate_recv.at[slot],
            device_id=(peer, layer),
            device_id_type=MESH,
        )

    def send_rate(k, carry):
        rate_copy(me, lax.rem(me + k, faces)).start()
        return carry

    lax.fori_loop(1, faces, send_rate, 0)
    surface = (layer == 0).astype(jnp.float32)
    share = surface * disc_rate / 3.0
    residual[0] = part_ref[0] + add_into([tri_ref[0, c] for c in range(3)], [share] * 3, rows, 3)

    def wait_rate(k, total):
        peer = lax.rem(me + k, faces)
        rate_copy(peer, peer).wait_recv()
        return total + landed[peer]

    own = spread[pl.ds(pl.multiple_of(me * SUB, SUB), SUB), :]
    pad_rate = -lax.fori_loop(1, faces, wait_rate, own)
    share = surface * pad_rate / 3.0
    residual[1] = part_ref[1] + add_into([tri_ref[1, c] for c in range(3)], [share] * 3, rows, 3)

    rim = rim_ref[...]
    at_rim = [
        pick(lambda r: row_spread(residual[body, r : r + 1, :], SUB), rows, rim) for body in range(2)
    ]
    rim_out[...] = jnp.where(line < 4, at_rim[0], at_rim[1])

    def rim_copy(slot, to):
        return pltpu.make_async_remote_copy(
            src_ref=rim_out,
            dst_ref=rim_in.at[slot],
            send_sem=rim_send.at[slot],
            recv_sem=rim_recv.at[slot],
            device_id=(me, to),
            device_id_type=MESH,
        )

    @pl.when(layer > 0)
    def _():
        rim_copy(1, layer - 1).start()

    @pl.when(layer < layers - 1)
    def _():
        rim_copy(0, layer + 1).start()

    @pl.when(layer == 0)
    def _():
        rim_in[0] = zeros

    @pl.when(layer == layers - 1)
    def _():
        rim_in[1] = zeros

    @pl.when(layer > 0)
    def _():
        rim_copy(0, layer - 1).wait_recv()

    @pl.when(layer < layers - 1)
    def _():
        rim_copy(1, layer + 1).wait_recv()

    from_below = jnp.concatenate([rim_in[0, 1:], rim_in[0, :1]], axis=0)
    from_above = jnp.concatenate([rim_in[1, SUB - 1 :], rim_in[1, : SUB - 1]], axis=0)
    more = jnp.where(jnp.bitwise_and(line, 1) == 0, from_below, from_above)
    for body in range(2):
        mine = (line < 4) if body == 0 else (line >= 4)
        got = add_into([rim], [jnp.where(mine, more, 0.0)], rows, 3)
        out_ref[body] = (
            field_ref[body] + increment_factor * (residual[body] + got) / storage_ref[body]
        )

    @pl.when(layer > 0)
    def _():
        rim_copy(1, layer - 1).wait_send()

    @pl.when(layer < layers - 1)
    def _():
        rim_copy(0, layer + 1).wait_send()

    def drain(k, carry):
        peer = lax.rem(me + k, faces)
        pad_copy(me, peer).wait_send()
        rate_copy(me, peer).wait_send()
        return carry

    lax.fori_loop(1, faces, drain, 0)


def local(
    faces,
    layers,
    thermal_field,
    lumped_storage,
    simplex_vertices,
    stiffness_entries,
    interface_vertices,
    touching_triangle_vertices,
    partner_lookup,
    engaged_flags,
    rotor_gap_quantities,
    lining_orthogonal_motion,
    touching_transfer_factor,
):
    nodes = thermal_field.shape[-1]
    rows = nodes // LANES
    tets = simplex_vertices.shape[-1]
    tiles = tets // LANES
    field = thermal_field.reshape(2, rows, LANES)
    storage = lumped_storage.reshape(2, rows, LANES)
    corners = (
        simplex_vertices.reshape(2, 4, tiles, LANES).transpose(0, 2, 1, 3).reshape(2, tiles * 4, LANES)
    )
    entries = stiffness_entries.reshape(2, 10, tiles, LANES)
    rim = (
        interface_vertices.reshape(2, 2, 2, LANES).transpose(0, 2, 1, 3).reshape(SUB, LANES)
    )
    tri = touching_triangle_vertices.reshape(2, 3, SUB, LANES)
    flags = engaged_flags.reshape(SUB, LANES)
    gaps = rotor_gap_quantities.reshape(3, SUB, LANES)
    motion = lining_orthogonal_motion.reshape(SUB, LANES)
    factor = touching_transfer_factor.reshape(SUB, LANES)
    vmem = pl.BlockSpec(memory_space=pltpu.VMEM)
    f32 = jnp.float32
    part = pl.pallas_call(
        element_kernel,
        out_shape=jax.ShapeDtypeStruct((2, rows, LANES), f32),
        in_specs=[vmem] * 3,
        out_specs=vmem,
        scratch_shapes=[pltpu.VMEM((2, rows, SUB, LANES), f32)],
        compiler_params=pltpu.CompilerParams(vmem_limit_bytes=32 * 1024 * 1024),
        name="element_part",
    )(field, corners, entries)
    advanced, pressure = pl.pallas_call(
        functools.partial(contact_kernel, faces, layers),
        out_shape=(
            jax.ShapeDtypeStruct((2, rows, LANES), f32),
            jax.ShapeDtypeStruct((SUB, LANES), f32),
        ),
        in_specs=[vmem] * 10,
        out_specs=(vmem, vmem),
        scratch_shapes=[
            pltpu.VMEM((2, rows, SUB, LANES), f32),
            pltpu.VMEM((2, rows, LANES), f32),
            pltpu.VMEM((faces, 2, SUB, LANES), f32),
            pltpu.VMEM((faces * SUB, LANES), f32),
            pltpu.VMEM((faces, SUB, LANES), f32),
            pltpu.VMEM((SUB, LANES), f32),
            pltpu.VMEM((2, SUB, LANES), f32),
            pltpu.SemaphoreType.DMA((faces,)),
            pltpu.SemaphoreType.DMA((faces,)),
            pltpu.SemaphoreType.DMA((faces,)),
            pltpu.SemaphoreType.DMA((faces,)),
            pltpu.SemaphoreType.DMA((2,)),
            pltpu.SemaphoreType.DMA((2,)),
        ],
        compiler_params=pltpu.CompilerParams(
            collective_id=0, has_side_effects=True, vmem_limit_bytes=32 * 1024 * 1024
        ),
        name="contact_part",
    )(field, storage, part, rim, tri, partner_lookup, flags, gaps, motion, factor)
    return (advanced.reshape(thermal_field.shape), pressure.reshape(engaged_flags.shape))


def solution(mesh):
    placed = (
        P(None, "face", "depth", None),
        P(None, "face", "depth", None),
        P(None, "face", "depth", None, None),
        P(None, "face", "depth", None, None),
        P(None, "face", "depth", None, None),
        P(None, "face", None, None),
        P(),
        P("face", None),
        P(None, "face", None),
        P("face", None),
        P("face", None),
    )
    return jax.shard_map(
        functools.partial(local, mesh.shape["face"], mesh.shape["depth"]),
        mesh=mesh,
        in_specs=placed,
        out_specs=(P(None, "face", "depth", None), P("face", None)),
        check_vma=False,
    )
```

```python
import functools

import jax
import jax.numpy as jnp
from jax import lax
from jax.experimental import pallas as pl
from jax.experimental.pallas import tpu as pltpu
from jax.sharding import PartitionSpec as P

increment_factor = 0.05
nitsche = 1.0
film_floor = 0.25

LANES = 128
SUB = 8
MESH = pl.DeviceIdType.MESH


def row_spread(row, count):
    return jnp.broadcast_to(row, (count, LANES))


def pick(row_of, rows, index):
    low = jnp.bitwise_and(index, LANES - 1)
    high = jnp.right_shift(index, 7)
    out = jnp.zeros(index.shape, jnp.float32)
    for r in range(rows):
        got = jnp.take_along_axis(row_of(r), low, axis=1, mode="promise_in_bounds")
        out = jnp.where(high == r, got, out)
    return out


def split(value, pieces):
    parts = []
    for _ in range(pieces - 1):
        head = value.astype(jnp.bfloat16).astype(jnp.float32)
        parts.append(head)
        value = value - head
    parts.append(value)
    return parts


def fold(both, rows, pieces):
    total = both[:rows]
    for k in range(1, pieces):
        total = total + both[k * rows : (k + 1) * rows]
    return total


def unturn(both, rows, pieces):
    wide = jnp.concatenate([both, jnp.zeros((LANES, LANES - rows * pieces), jnp.float32)], axis=1)
    return fold(wide.T, rows, pieces)


def add_into(indices, values, rows, pieces, turned=False):
    lane_iota = lax.broadcasted_iota(jnp.int32, (LANES, LANES), 0).astype(jnp.float32).astype(jnp.bfloat16)
    row_iota = lax.broadcasted_iota(jnp.int32, (rows, LANES), 0).astype(jnp.float32).astype(jnp.bfloat16)
    one = jnp.ones((LANES, LANES), jnp.bfloat16)
    zero = jnp.zeros((LANES, LANES), jnp.bfloat16)
    zero_rows = jnp.zeros((rows, LANES), jnp.bfloat16)
    left = [[] for _ in range(pieces)]
    right = []
    for index, value in zip(indices, values):
        low = jnp.bitwise_and(index, LANES - 1).astype(jnp.float32)
        high = jnp.right_shift(index, 7).astype(jnp.float32)
        parts = split(value, pieces)

        def wide(array, s, count):
            base = row_spread(array[s : s + 1, :], 16).astype(jnp.bfloat16)
            return jnp.concatenate([base] * (count // 16), axis=0) if count > 16 else base

        for s in range(SUB):
            right.append(jnp.where(lane_iota == wide(low, s, LANES), one, zero))
            hit = row_iota == wide(high, s, rows)
            for k in range(pieces):
                left[k].append(jnp.where(hit, wide(parts[k], s, rows), zero_rows))
    left = jnp.concatenate([jnp.concatenate(one_piece, axis=1) for one_piece in left], axis=0)
    right = jnp.concatenate(right, axis=1)
    contract = (((1,), (1,)), ((), ()))
    if turned:
        return lax.dot_general(right, left, contract, preferred_element_type=jnp.float32)
    both = lax.dot_general(left, right, contract, preferred_element_type=jnp.float32)
    return fold(both, rows, pieces)


def spread_table(field_ref, table, body, rows):
    for r in range(rows):
        table[body, r] = row_spread(field_ref[body, r : r + 1, :], SUB)


def element_steps(table, corners_ref, entries_ref, rows, sums, start, stop):
    chunks = entries_ref.shape[2] // SUB

    def step(i, carry):
        body = i // chunks
        j = lax.rem(i, chunks)
        first = pl.multiple_of(j * (4 * SUB), 4 * SUB)
        tile = pl.multiple_of(j * SUB, SUB)
        index = [corners_ref[body, pl.ds(first + c, SUB, stride=4), :] for c in range(4)]
        t = [pick(lambda r: table[body, r], rows, index[c]) for c in range(4)]
        k = [entries_ref[body, m, pl.ds(tile, SUB), :] for m in range(10)]
        out = [
            -(k[0] * t[0] + k[4] * t[1] + k[5] * t[2] + k[6] * t[3]),
            -(k[4] * t[0] + k[1] * t[1] + k[7] * t[2] + k[8] * t[3]),
            -(k[5] * t[0] + k[7] * t[1] + k[2] * t[2] + k[9] * t[3]),
            -(k[6] * t[0] + k[8] * t[1] + k[9] * t[2] + k[3] * t[3]),
        ]
        sums[body] += add_into(index, out, rows, 2, turned=True)
        return carry

    lax.fori_loop(start, stop, step, 0)


def step_kernel(
    faces,
    layers,
    field_hbm,
    storage_hbm,
    corners_hbm,
    entries_hbm,
    rim_hbm,
    tri_hbm,
    match_hbm,
    flag_hbm,
    gap_hbm,
    motion_hbm,
    factor_hbm,
    out_ref,
    pressure_ref,
    field_ref,
    storage_ref,
    corners_ref,
    entries_ref,
    rim_ref,
    tri_ref,
    match_ref,
    flag_ref,
    gap_ref,
    motion_ref,
    factor_ref,
    load,
    table,
    sums,
    residual,
    pad,
    spread,
    landed,
    rim_out,
    rim_in,
    pad_send,
    pad_recv,
    rate_send,
    rate_recv,
    rim_send,
    rim_recv,
):
    rows = field_ref.shape[1]
    me = lax.axis_index("face")
    layer = lax.axis_index("depth")

    def fetch(k, source, target):
        copy = pltpu.make_async_copy(source, target, load.at[k])
        copy.start()
        return copy

    get_field = fetch(0, field_hbm, field_ref)
    get_tri = fetch(1, tri_hbm, tri_ref)
    get_motion = fetch(2, motion_hbm, motion_ref)
    get_corners = [fetch(3, corners_hbm.at[0], corners_ref.at[0])]
    get_entries = [fetch(4, entries_hbm.at[0], entries_ref.at[0])]
    get_corners.append(fetch(5, corners_hbm.at[1], corners_ref.at[1]))
    get_entries.append(fetch(6, entries_hbm.at[1], entries_ref.at[1]))
    get_rim = fetch(7, rim_hbm, rim_ref)
    get_rest = [
        fetch(8, match_hbm, match_ref),
        fetch(9, flag_hbm, flag_ref),
        fetch(10, gap_hbm, gap_ref),
        fetch(11, factor_hbm, factor_ref),
        fetch(12, storage_hbm, storage_ref),
    ]

    barrier = pltpu.get_barrier_semaphore()

    def greet(k, carry):
        peer = lax.rem(me + k, faces)
        pl.semaphore_signal(barrier, inc=1, device_id=(peer, layer), device_id_type=MESH)
        return carry

    lax.fori_loop(1, faces, greet, 0)

    @pl.when(layer > 0)
    def _():
        pl.semaphore_signal(barrier, inc=1, device_id=(me, layer - 1), device_id_type=MESH)

    @pl.when(layer < layers - 1)
    def _():
        pl.semaphore_signal(barrier, inc=1, device_id=(me, layer + 1), device_id_type=MESH)

    sums[...] = jnp.zeros_like(sums)
    get_field.wait()
    get_tri.wait()
    get_motion.wait()
    traces = []
    for body in range(2):
        spread_table(field_ref, table, body, rows)
        t = [pick(lambda r: table[body, r], rows, tri_ref[body, c]) for c in range(3)]
        traces.append((t[0] + t[1] + t[2]) / 3.0)
    pad[me, 0] = motion_ref[...]
    pad[me, 1] = traces[1]

    steps = 2 * (entries_ref.shape[2] // SUB)
    cuts = (0, steps // 4, steps * 5 // 8, steps)

    def elements(part):
        element_steps(table, corners_ref, entries_ref, rows, sums, cuts[part], cuts[part + 1])

    get_corners[0].wait()
    get_entries[0].wait()
    elements(0)

    around = (layer > 0).astype(jnp.int32) + (layer < layers - 1).astype(jnp.int32)
    pl.semaphore_wait(barrier, faces - 1 + around)

    def pad_copy(slot, peer):
        return pltpu.make_async_remote_copy(
            src_ref=pad.at[slot],
            dst_ref=pad.at[slot],
            send_sem=pad_send.at[peer],
            recv_sem=pad_recv.at[slot],
            device_id=(peer, layer),
            device_id_type=MESH,
        )

    def send_pad(k, carry):
        pad_copy(me, lax.rem(me + k, faces)).start()
        return carry

    lax.fori_loop(1, faces, send_pad, 0)

    get_corners[1].wait()
    get_entries[1].wait()
    elements(1)
    for one in get_rest:
        one.wait()
    get_rim.wait()

    rim = rim_ref[...]
    line = lax.broadcasted_iota(jnp.int32, (SUB, LANES), 0)
    column = lax.broadcasted_iota(jnp.int32, (SUB, LANES), 1)
    both_rows = 2 * rows
    absent = SUB * LANES
    shift = jnp.where(line < SUB // 2, 0, rows * LANES)
    slot = line * LANES + column - absent
    where_rim = add_into([rim + shift], [slot.astype(jnp.float32)], both_rows, 2)
    where_rim = where_rim.astype(jnp.int32) + absent

    band = pl.multiple_of(me // SUB * SUB, SUB)
    mine = line == lax.rem(me, SUB)
    match = jnp.concatenate(
        [
            jnp.sum(
                jnp.where(mine, match_ref[pl.ds(band, SUB), s * LANES : (s + 1) * LANES], 0),
                axis=0,
                keepdims=True,
            )
            for s in range(SUB)
        ],
        axis=0,
    )
    low = jnp.bitwise_and(match, LANES - 1)
    high = jnp.right_shift(match, 7)

    def wait_pad(k, carry):
        peer = lax.rem(me + k, faces)
        pad_copy(peer, peer).wait_recv()
        return carry

    lax.fori_loop(1, faces, wait_pad, 0)

    def look(patch, carry):
        normal, trace = carry
        for s in range(SUB):
            hit = high == patch * SUB + s
            for_normal = row_spread(pad[patch, 0, s : s + 1, :], SUB)
            for_trace = row_spread(pad[patch, 1, s : s + 1, :], SUB)
            normal = jnp.where(
                hit, jnp.take_along_axis(for_normal, low, axis=1, mode="promise_in_bounds"), normal
            )
            trace = jnp.where(
                hit, jnp.take_along_axis(for_trace, low, axis=1, mode="promise_in_bounds"), trace
            )
        return normal, trace

    zeros = jnp.zeros((SUB, LANES), jnp.float32)
    normal, trace = lax.fori_loop(0, faces, look, (zeros, zeros))
    active = flag_ref[...].astype(jnp.float32)
    pressure = active * jnp.maximum(gap_ref[2] + nitsche * (gap_ref[0] - normal - gap_ref[1]), 0.0)
    pressure_ref[...] = pressure
    disc_rate = active * factor_ref[...] * (film_floor + pressure) * (trace - traces[0])
    spread[...] = add_into([match], [disc_rate], faces * SUB, 3)

    def rate_copy(slot, peer):
        return pltpu.make_async_remote_copy(
            src_ref=spread.at[pl.ds(pl.multiple_of(peer * SUB, SUB), SUB)],
            dst_ref=landed.at[slot],
            send_sem=rate_send.at[peer],
            recv_sem=rate_recv.at[slot],
            device_id=(peer, layer),
            device_id_type=MESH,
        )

    def send_rate(k, carry):
        rate_copy(me, lax.rem(me + k, faces)).start()
        return carry

    lax.fori_loop(1, faces, send_rate, 0)
    surface = (layer == 0).astype(jnp.float32)
    share = surface * disc_rate / 3.0
    residual[0] = add_into([tri_ref[0, c] for c in range(3)], [share] * 3, rows, 3)

    elements(2)

    def wait_rate(k, total):
        peer = lax.rem(me + k, faces)
        rate_copy(peer, peer).wait_recv()
        return total + landed[peer]

    own = spread[pl.ds(pl.multiple_of(me * SUB, SUB), SUB), :]
    pad_rate = -lax.fori_loop(1, faces, wait_rate, own)
    share = surface * pad_rate / 3.0
    residual[1] = add_into([tri_ref[1, c] for c in range(3)], [share] * 3, rows, 3)
    for body in range(2):
        residual[body] += unturn(sums[body], rows, 2)

    at_rim = [
        pick(lambda r: row_spread(residual[body, r : r + 1, :], SUB), rows, rim) for body in range(2)
    ]
    rim_out[...] = jnp.where(line < SUB // 2, at_rim[0], at_rim[1])

    def rim_copy(slot, to):
        return pltpu.make_async_remote_copy(
            src_ref=rim_out,
            dst_ref=rim_in.at[slot],
            send_sem=rim_send.at[slot],
            recv_sem=rim_recv.at[slot],
            device_id=(me, to),
            device_id_type=MESH,
        )

    @pl.when(layer > 0)
    def _():
        rim_copy(1, layer - 1).start()

    @pl.when(layer < layers - 1)
    def _():
        rim_copy(0, layer + 1).start()

    @pl.when(layer == 0)
    def _():
        rim_in[0] = zeros

    @pl.when(layer == layers - 1)
    def _():
        rim_in[1] = zeros

    def drain(k, carry):
        peer = lax.rem(me + k, faces)
        pad_copy(me, peer).wait_send()
        rate_copy(me, peer).wait_send()
        return carry

    lax.fori_loop(1, faces, drain, 0)

    @pl.when(layer > 0)
    def _():
        rim_copy(0, layer - 1).wait_recv()

    @pl.when(layer < layers - 1)
    def _():
        rim_copy(1, layer + 1).wait_recv()

    from_below = jnp.concatenate([rim_in[0, 1:], rim_in[0, :1]], axis=0)
    from_above = jnp.concatenate([rim_in[1, SUB - 1 :], rim_in[1, : SUB - 1]], axis=0)
    more = jnp.where(jnp.bitwise_and(line, 1) == 0, from_below, from_above)
    more_rows = [row_spread(more[s : s + 1, :], SUB) for s in range(SUB)]
    for body in range(2):
        for part in range(rows // SUB):
            at = body * rows + part * SUB
            got = pick(lambda s: more_rows[s], SUB, where_rim[at : at + SUB])
            here = slice(part * SUB, (part + 1) * SUB)
            out_ref[body, here] = (
                field_ref[body, here]
                + increment_factor * (residual[body, here] + got) / storage_ref[body, here]
            )

    @pl.when(layer > 0)
    def _():
        rim_copy(1, layer - 1).wait_send()

    @pl.when(layer < layers - 1)
    def _():
        rim_copy(0, layer + 1).wait_send()


def local(
    faces,
    layers,
    thermal_field,
    lumped_storage,
    simplex_vertices,
    stiffness_entries,
    interface_vertices,
    touching_triangle_vertices,
    partner_lookup,
    engaged_flags,
    rotor_gap_quantities,
    lining_orthogonal_motion,
    touching_transfer_factor,
):
    nodes = thermal_field.shape[-1]
    rows = nodes // LANES
    tets = simplex_vertices.shape[-1]
    tiles = tets // LANES
    field = thermal_field.reshape(2, rows, LANES)
    storage = lumped_storage.reshape(2, rows, LANES)
    corners = (
        simplex_vertices.reshape(2, 4, tiles, LANES).transpose(0, 2, 1, 3).reshape(2, tiles * 4, LANES)
    )
    entries = stiffness_entries.reshape(2, 10, tiles, LANES)
    rim = (
        interface_vertices.reshape(2, 2, 2, LANES).transpose(0, 2, 1, 3).reshape(SUB, LANES)
    )
    tri = touching_triangle_vertices.reshape(2, 3, SUB, LANES)
    flags = engaged_flags.reshape(SUB, LANES)
    gaps = rotor_gap_quantities.reshape(3, SUB, LANES)
    motion = lining_orthogonal_motion.reshape(SUB, LANES)
    factor = touching_transfer_factor.reshape(SUB, LANES)
    vmem = pl.BlockSpec(memory_space=pltpu.VMEM)
    f32 = jnp.float32
    arrays = (field, storage, corners, entries, rim, tri, partner_lookup, flags, gaps, motion, factor)
    advanced, pressure = pl.pallas_call(
        functools.partial(step_kernel, faces, layers),
        out_shape=(
            jax.ShapeDtypeStruct((2, rows, LANES), f32),
            jax.ShapeDtypeStruct((SUB, LANES), f32),
        ),
        in_specs=[pl.BlockSpec(memory_space=pltpu.HBM)] * len(arrays),
        out_specs=(vmem, vmem),
        scratch_shapes=[pltpu.VMEM(array.shape, array.dtype) for array in arrays]
        + [
            pltpu.SemaphoreType.DMA((13,)),
            pltpu.VMEM((2, rows, SUB, LANES), f32),
            pltpu.VMEM((2, LANES, 2 * rows), f32),
            pltpu.VMEM((2, rows, LANES), f32),
            pltpu.VMEM((faces, 2, SUB, LANES), f32),
            pltpu.VMEM((faces * SUB, LANES), f32),
            pltpu.VMEM((faces, SUB, LANES), f32),
            pltpu.VMEM((SUB, LANES), f32),
            pltpu.VMEM((2, SUB, LANES), f32),
            pltpu.SemaphoreType.DMA((faces,)),
            pltpu.SemaphoreType.DMA((faces,)),
            pltpu.SemaphoreType.DMA((faces,)),
            pltpu.SemaphoreType.DMA((faces,)),
            pltpu.SemaphoreType.DMA((2,)),
            pltpu.SemaphoreType.DMA((2,)),
        ],
        compiler_params=pltpu.CompilerParams(
            collective_id=0, has_side_effects=True, vmem_limit_bytes=60 * 1024 * 1024
        ),
        name="thermal_step",
    )(*arrays)
    return (advanced.reshape(thermal_field.shape), pressure.reshape(engaged_flags.shape))


def solution(mesh):
    placed = (
        P(None, "face", "depth", None),
        P(None, "face", "depth", None),
        P(None, "face", "depth", None, None),
        P(None, "face", "depth", None, None),
        P(None, "face", "depth", None, None),
        P(None, "face", None, None),
        P(),
        P("face", None),
        P(None, "face", None),
        P("face", None),
        P("face", None),
    )
    return jax.shard_map(
        functools.partial(local, mesh.shape["face"], mesh.shape["depth"]),
        mesh=mesh,
        in_specs=placed,
        out_specs=(P(None, "face", "depth", None), P("face", None)),
        check_vma=False,
    )
```

```python
import functools

import jax
import jax.numpy as jnp
from jax import lax
from jax.experimental import pallas as pl
from jax.experimental.pallas import tpu as pltpu
from jax.sharding import PartitionSpec as P

increment_factor = 0.05
nitsche = 1.0
film_floor = 0.25

LANES = 128
SUB = 8
MESH = pl.DeviceIdType.MESH


def row_spread(row, count):
    return jnp.broadcast_to(row, (count, LANES))


def pick(row_of, rows, index):
    low = jnp.bitwise_and(index, LANES - 1)
    high = jnp.right_shift(index, 7)
    out = jnp.zeros(index.shape, jnp.float32)
    for r in range(rows):
        got = jnp.take_along_axis(row_of(r), low, axis=1, mode="promise_in_bounds")
        out = jnp.where(high == r, got, out)
    return out


def split(value, pieces):
    parts = []
    for _ in range(pieces - 1):
        head = value.astype(jnp.bfloat16).astype(jnp.float32)
        parts.append(head)
        value = value - head
    parts.append(value)
    return parts


def fold(both, rows, pieces):
    total = both[:rows]
    for k in range(1, pieces):
        total = total + both[k * rows : (k + 1) * rows]
    return total


def join(both, rows, pieces):
    total = fold(both, 2 * rows, pieces)
    return jnp.concatenate([total[:rows], total[rows:]], axis=1)


def add_into(indices, values, rows, pieces, halves=True):
    lanes = LANES // 2 if halves else LANES
    lines = 2 * rows if halves else rows
    lane_iota = lax.broadcasted_iota(jnp.int32, (lanes, LANES), 0).astype(jnp.float32).astype(jnp.bfloat16)
    line_iota = lax.broadcasted_iota(jnp.int32, (lines, LANES), 0).astype(jnp.float32).astype(jnp.bfloat16)
    one = jnp.ones((lanes, LANES), jnp.bfloat16)
    zero = jnp.zeros((lanes, LANES), jnp.bfloat16)
    zero_lines = jnp.zeros((lines, LANES), jnp.bfloat16)
    left = [[] for _ in range(pieces)]
    right = []
    for index, value in zip(indices, values):
        low = jnp.bitwise_and(index, lanes - 1).astype(jnp.float32)
        high = jnp.right_shift(index, 7)
        if halves:
            high = high + jnp.bitwise_and(jnp.right_shift(index, 6), 1) * rows
        high = high.astype(jnp.float32)
        parts = split(value, pieces)

        def wide(array, s, count):
            base = row_spread(array[s : s + 1, :], 16).astype(jnp.bfloat16)
            return jnp.concatenate([base] * (count // 16), axis=0)

        for s in range(SUB):
            right.append(jnp.where(lane_iota == wide(low, s, lanes), one, zero))
            hit = line_iota == wide(high, s, lines)
            for k in range(pieces):
                left[k].append(jnp.where(hit, wide(parts[k], s, lines), zero_lines))
    left = jnp.concatenate([jnp.concatenate(one_piece, axis=1) for one_piece in left], axis=0)
    right = jnp.concatenate(right, axis=1)
    both = lax.dot_general(left, right, (((1,), (1,)), ((), ())), preferred_element_type=jnp.float32)
    return both if halves else fold(both, rows, pieces)


def spread_table(field_ref, table, body, rows):
    for r in range(rows):
        table[body, r] = row_spread(field_ref[body, r : r + 1, :], SUB)


def element_step(i, table, corners_ref, entries_ref, rows, sums):
    chunks = entries_ref.shape[2] // SUB
    body = i // chunks
    j = lax.rem(i, chunks)
    first = pl.multiple_of(j * (4 * SUB), 4 * SUB)
    tile = pl.multiple_of(j * SUB, SUB)
    index = [corners_ref[body, pl.ds(first + c, SUB, stride=4), :] for c in range(4)]
    t = [pick(lambda r: table[body, r], rows, index[c]) for c in range(4)]
    k = [entries_ref[body, m, pl.ds(tile, SUB), :] for m in range(10)]
    out = [
        -(k[0] * t[0] + k[4] * t[1] + k[5] * t[2] + k[6] * t[3]),
        -(k[4] * t[0] + k[1] * t[1] + k[7] * t[2] + k[8] * t[3]),
        -(k[5] * t[0] + k[7] * t[1] + k[2] * t[2] + k[9] * t[3]),
        -(k[6] * t[0] + k[8] * t[1] + k[9] * t[2] + k[3] * t[3]),
    ]
    sums[body] += add_into(index, out, rows, 2)


def step_kernel(
    faces,
    layers,
    field_hbm,
    storage_hbm,
    corners_hbm,
    entries_hbm,
    rim_hbm,
    tri_hbm,
    match_hbm,
    flag_hbm,
    gap_hbm,
    motion_hbm,
    factor_hbm,
    out_ref,
    pressure_ref,
    field_ref,
    storage_ref,
    corners_ref,
    entries_ref,
    rim_ref,
    tri_ref,
    match_ref,
    flag_ref,
    gap_ref,
    motion_ref,
    factor_ref,
    load,
    disc_trace,
    rates,
    table,
    sums,
    residual,
    pad,
    spread,
    landed,
    rim_out,
    rim_in,
    pad_send,
    pad_recv,
    rate_send,
    rate_recv,
    rim_send,
    rim_recv,
):
    rows = field_ref.shape[1]
    me = lax.axis_index("face")
    layer = lax.axis_index("depth")

    def fetch(k, source, target):
        copy = pltpu.make_async_copy(source, target, load.at[k])
        copy.start()
        return copy

    get_field = fetch(0, field_hbm, field_ref)
    get_tri = fetch(1, tri_hbm, tri_ref)
    get_motion = fetch(2, motion_hbm, motion_ref)
    get_corners = [fetch(3, corners_hbm.at[0], corners_ref.at[0])]
    get_entries = [fetch(4, entries_hbm.at[0], entries_ref.at[0])]
    get_corners.append(fetch(5, corners_hbm.at[1], corners_ref.at[1]))
    get_entries.append(fetch(6, entries_hbm.at[1], entries_ref.at[1]))
    get_rim = fetch(7, rim_hbm, rim_ref)
    get_rest = [
        fetch(8, match_hbm, match_ref),
        fetch(9, flag_hbm, flag_ref),
        fetch(10, gap_hbm, gap_ref),
        fetch(11, factor_hbm, factor_ref),
        fetch(12, storage_hbm, storage_ref),
    ]

    barrier = pltpu.get_barrier_semaphore()

    def greet(k, carry):
        peer = lax.rem(me + k, faces)
        pl.semaphore_signal(barrier, inc=1, device_id=(peer, layer), device_id_type=MESH)
        return carry

    lax.fori_loop(1, faces, greet, 0)

    @pl.when(layer > 0)
    def _():
        pl.semaphore_signal(barrier, inc=1, device_id=(me, layer - 1), device_id_type=MESH)

    @pl.when(layer < layers - 1)
    def _():
        pl.semaphore_signal(barrier, inc=1, device_id=(me, layer + 1), device_id_type=MESH)

    sums[...] = jnp.zeros_like(sums)
    get_field.wait()
    get_tri.wait()
    get_motion.wait()
    for body in range(2):
        spread_table(field_ref, table, body, rows)
        t = [pick(lambda r: table[body, r], rows, tri_ref[body, c]) for c in range(3)]
        trace = (t[0] + t[1] + t[2]) / 3.0
        if body == 0:
            disc_trace[...] = trace
        else:
            pad[me, 1] = trace
    pad[me, 0] = motion_ref[...]
    around = (layer > 0).astype(jnp.int32) + (layer < layers - 1).astype(jnp.int32)
    line = lax.broadcasted_iota(jnp.int32, (SUB, LANES), 0)
    column = lax.broadcasted_iota(jnp.int32, (SUB, LANES), 1)
    zeros = jnp.zeros((SUB, LANES), jnp.float32)

    def pad_copy(slot, peer):
        return pltpu.make_async_remote_copy(
            src_ref=pad.at[slot],
            dst_ref=pad.at[slot],
            send_sem=pad_send.at[peer],
            recv_sem=pad_recv.at[slot],
            device_id=(peer, layer),
            device_id_type=MESH,
        )

    def send_pad(k, carry):
        pad_copy(me, lax.rem(me + k, faces)).start()
        return carry

    def wait_pad(k, carry):
        peer = lax.rem(me + k, faces)
        pad_copy(peer, peer).wait_recv()
        return carry

    def rate_copy(slot, peer):
        return pltpu.make_async_remote_copy(
            src_ref=spread.at[pl.ds(pl.multiple_of(peer * SUB, SUB), SUB)],
            dst_ref=landed.at[slot],
            send_sem=rate_send.at[peer],
            recv_sem=rate_recv.at[slot],
            device_id=(peer, layer),
            device_id_type=MESH,
        )

    def send_rate(k, carry):
        rate_copy(me, lax.rem(me + k, faces)).start()
        return carry

    def rate_faces():
        band = pl.multiple_of(me // SUB * SUB, SUB)
        mine = line == lax.rem(me, SUB)
        match = jnp.concatenate(
            [
                jnp.sum(
                    jnp.where(mine, match_ref[pl.ds(band, SUB), s * LANES : (s + 1) * LANES], 0),
                    axis=0,
                    keepdims=True,
                )
                for s in range(SUB)
            ],
            axis=0,
        )
        low = jnp.bitwise_and(match, LANES - 1)
        high = jnp.right_shift(match, 7)

        def look(patch, carry):
            normal, trace = carry
            for s in range(SUB):
                hit = high == patch * SUB + s
                for_normal = row_spread(pad[patch, 0, s : s + 1, :], SUB)
                for_trace = row_spread(pad[patch, 1, s : s + 1, :], SUB)
                normal = jnp.where(
                    hit, jnp.take_along_axis(for_normal, low, axis=1, mode="promise_in_bounds"), normal
                )
                trace = jnp.where(
                    hit, jnp.take_along_axis(for_trace, low, axis=1, mode="promise_in_bounds"), trace
                )
            return normal, trace

        normal, trace = lax.fori_loop(0, faces, look, (zeros, zeros))
        active = flag_ref[...].astype(jnp.float32)
        pressure = active * jnp.maximum(gap_ref[2] + nitsche * (gap_ref[0] - normal - gap_ref[1]), 0.0)
        pressure_ref[...] = pressure
        rate = active * factor_ref[...] * (film_floor + pressure) * (trace - disc_trace[...])
        rates[0] = rate
        spread[...] = add_into([match], [rate], faces * SUB, 3, halves=False)

    get_corners[0].wait()
    get_entries[0].wait()
    chunks = entries_ref.shape[2] // SUB
    steps = 2 * chunks

    def run(i, carry):
        @pl.when(i == steps // 8)
        def _():
            pl.semaphore_wait(barrier, faces - 1 + around)
            lax.fori_loop(1, faces, send_pad, 0)

        @pl.when(i == chunks)
        def _():
            get_corners[1].wait()
            get_entries[1].wait()

        @pl.when(i == steps * 5 // 8)
        def _():
            for one in get_rest:
                one.wait()
            lax.fori_loop(1, faces, wait_pad, 0)
            rate_faces()
            lax.fori_loop(1, faces, send_rate, 0)

        element_step(i, table, corners_ref, entries_ref, rows, sums)
        return carry

    lax.fori_loop(0, steps, run, 0)

    get_rim.wait()
    rim = rim_ref[...]
    absent = SUB * LANES
    shift = jnp.where(line < SUB // 2, 0, rows * LANES)
    slot = line * LANES + column - absent
    where_rim = join(add_into([rim + shift], [slot.astype(jnp.float32)], 2 * rows, 2), 2 * rows, 2)
    where_rim = where_rim.astype(jnp.int32) + absent

    def wait_rate(k, total):
        peer = lax.rem(me + k, faces)
        rate_copy(peer, peer).wait_recv()
        return total + landed[peer]

    own = spread[pl.ds(pl.multiple_of(me * SUB, SUB), SUB), :]
    rates[1] = -lax.fori_loop(1, faces, wait_rate, own)
    surface = (layer == 0).astype(jnp.float32)

    def finish(body, carry):
        share = surface * rates[body] / 3.0
        contact = add_into([tri_ref[body, c] for c in range(3)], [share] * 3, rows, 3)
        residual[body] = join(contact, rows, 3) + join(sums[body], rows, 2)
        return carry

    lax.fori_loop(0, 2, finish, 0)

    at_rim = [
        pick(lambda r: row_spread(residual[body, r : r + 1, :], SUB), rows, rim) for body in range(2)
    ]
    rim_out[...] = jnp.where(line < SUB // 2, at_rim[0], at_rim[1])

    def rim_copy(slot, to):
        return pltpu.make_async_remote_copy(
            src_ref=rim_out,
            dst_ref=rim_in.at[slot],
            send_sem=rim_send.at[slot],
            recv_sem=rim_recv.at[slot],
            device_id=(me, to),
            device_id_type=MESH,
        )

    @pl.when(layer > 0)
    def _():
        rim_copy(1, layer - 1).start()

    @pl.when(layer < layers - 1)
    def _():
        rim_copy(0, layer + 1).start()

    @pl.when(layer == 0)
    def _():
        rim_in[0] = zeros

    @pl.when(layer == layers - 1)
    def _():
        rim_in[1] = zeros

    def drain(k, carry):
        peer = lax.rem(me + k, faces)
        pad_copy(me, peer).wait_send()
        rate_copy(me, peer).wait_send()
        return carry

    lax.fori_loop(1, faces, drain, 0)

    @pl.when(layer > 0)
    def _():
        rim_copy(0, layer - 1).wait_recv()

    @pl.when(layer < layers - 1)
    def _():
        rim_copy(1, layer + 1).wait_recv()

    from_below = jnp.concatenate([rim_in[0, 1:], rim_in[0, :1]], axis=0)
    from_above = jnp.concatenate([rim_in[1, SUB - 1 :], rim_in[1, : SUB - 1]], axis=0)
    more = jnp.where(jnp.bitwise_and(line, 1) == 0, from_below, from_above)
    more_rows = [row_spread(more[s : s + 1, :], SUB) for s in range(SUB)]
    for body in range(2):
        for part in range(rows // SUB):
            at = body * rows + part * SUB
            got = pick(lambda s: more_rows[s], SUB, where_rim[at : at + SUB])
            here = slice(part * SUB, (part + 1) * SUB)
            out_ref[body, here] = (
                field_ref[body, here]
                + increment_factor * (residual[body, here] + got) / storage_ref[body, here]
            )

    @pl.when(layer > 0)
    def _():
        rim_copy(1, layer - 1).wait_send()

    @pl.when(layer < layers - 1)
    def _():
        rim_copy(0, layer + 1).wait_send()


def local(
    faces,
    layers,
    thermal_field,
    lumped_storage,
    simplex_vertices,
    stiffness_entries,
    interface_vertices,
    touching_triangle_vertices,
    partner_lookup,
    engaged_flags,
    rotor_gap_quantities,
    lining_orthogonal_motion,
    touching_transfer_factor,
):
    nodes = thermal_field.shape[-1]
    rows = nodes // LANES
    tets = simplex_vertices.shape[-1]
    tiles = tets // LANES
    field = thermal_field.reshape(2, rows, LANES)
    storage = lumped_storage.reshape(2, rows, LANES)
    corners = (
        simplex_vertices.reshape(2, 4, tiles, LANES).transpose(0, 2, 1, 3).reshape(2, tiles * 4, LANES)
    )
    entries = stiffness_entries.reshape(2, 10, tiles, LANES)
    rim = (
        interface_vertices.reshape(2, 2, 2, LANES).transpose(0, 2, 1, 3).reshape(SUB, LANES)
    )
    tri = touching_triangle_vertices.reshape(2, 3, SUB, LANES)
    flags = engaged_flags.reshape(SUB, LANES)
    gaps = rotor_gap_quantities.reshape(3, SUB, LANES)
    motion = lining_orthogonal_motion.reshape(SUB, LANES)
    factor = touching_transfer_factor.reshape(SUB, LANES)
    vmem = pl.BlockSpec(memory_space=pltpu.VMEM)
    f32 = jnp.float32
    arrays = (field, storage, corners, entries, rim, tri, partner_lookup, flags, gaps, motion, factor)
    advanced, pressure = pl.pallas_call(
        functools.partial(step_kernel, faces, layers),
        out_shape=(
            pltpu.VMEM((2, rows, LANES), f32),
            pltpu.VMEM((SUB, LANES), f32),
        ),
        in_specs=[pl.BlockSpec(memory_space=pltpu.HBM)] * len(arrays),
        out_specs=(vmem, vmem),
        scratch_shapes=[pltpu.VMEM(array.shape, array.dtype) for array in arrays]
        + [
            pltpu.SemaphoreType.DMA((13,)),
            pltpu.VMEM((SUB, LANES), f32),
            pltpu.VMEM((2, SUB, LANES), f32),
            pltpu.VMEM((2, rows, SUB, LANES), f32),
            pltpu.VMEM((2, 4 * rows, LANES // 2), f32),
            pltpu.VMEM((2, rows, LANES), f32),
            pltpu.VMEM((faces, 2, SUB, LANES), f32),
            pltpu.VMEM((faces * SUB, LANES), f32),
            pltpu.VMEM((faces, SUB, LANES), f32),
            pltpu.VMEM((SUB, LANES), f32),
            pltpu.VMEM((2, SUB, LANES), f32),
            pltpu.SemaphoreType.DMA((faces,)),
            pltpu.SemaphoreType.DMA((faces,)),
            pltpu.SemaphoreType.DMA((faces,)),
            pltpu.SemaphoreType.DMA((faces,)),
            pltpu.SemaphoreType.DMA((2,)),
            pltpu.SemaphoreType.DMA((2,)),
        ],
        compiler_params=pltpu.CompilerParams(
            collective_id=0, has_side_effects=True, vmem_limit_bytes=60 * 1024 * 1024
        ),
        name="thermal_step",
    )(*arrays)
    return (advanced.reshape(thermal_field.shape), pressure.reshape(engaged_flags.shape))


def solution(mesh):
    placed = (
        P(None, "face", "depth", None),
        P(None, "face", "depth", None),
        P(None, "face", "depth", None, None),
        P(None, "face", "depth", None, None),
        P(None, "face", "depth", None, None),
        P(None, "face", None, None),
        P(),
        P("face", None),
        P(None, "face", None),
        P("face", None),
        P("face", None),
    )
    return jax.shard_map(
        functools.partial(local, mesh.shape["face"], mesh.shape["depth"]),
        mesh=mesh,
        in_specs=placed,
        out_specs=(P(None, "face", "depth", None), P("face", None)),
        check_vma=False,
    )
```

```python
import functools

import jax
import jax.numpy as jnp
from jax import lax
from jax.experimental import pallas as pl
from jax.experimental.pallas import tpu as pltpu
from jax.sharding import PartitionSpec as P

increment_factor = 0.05
nitsche = 1.0
film_floor = 0.25

LANES = 128
SUB = 8
MESH = pl.DeviceIdType.MESH


def row_spread(row, count):
    return jnp.broadcast_to(row, (count, LANES))


def pick(row_of, rows, index):
    low = jnp.bitwise_and(index, LANES - 1)
    high = jnp.right_shift(index, 7)
    out = jnp.zeros(index.shape, jnp.float32)
    for r in range(rows):
        got = jnp.take_along_axis(row_of(r), low, axis=1, mode="promise_in_bounds")
        out = jnp.where(high == r, got, out)
    return out


def split(value, pieces):
    parts = []
    for _ in range(pieces - 1):
        head = value.astype(jnp.bfloat16).astype(jnp.float32)
        parts.append(head)
        value = value - head
    parts.append(value)
    return parts


def fold(both, rows, pieces):
    total = both[:rows]
    for k in range(1, pieces):
        total = total + both[k * rows : (k + 1) * rows]
    return total


def join(both, rows, pieces):
    total = fold(both, 2 * rows, pieces)
    return jnp.concatenate([total[:rows], total[rows:]], axis=1)


def add_into(indices, values, rows, pieces, halves=True):
    lanes = LANES // 2 if halves else LANES
    lines = 2 * rows if halves else rows
    lane_iota = lax.broadcasted_iota(jnp.int32, (lanes, LANES), 0).astype(jnp.float32).astype(jnp.bfloat16)
    line_iota = lax.broadcasted_iota(jnp.int32, (lines, LANES), 0).astype(jnp.float32).astype(jnp.bfloat16)
    one = jnp.ones((lanes, LANES), jnp.bfloat16)
    zero = jnp.zeros((lanes, LANES), jnp.bfloat16)
    zero_lines = jnp.zeros((lines, LANES), jnp.bfloat16)
    left = [[] for _ in range(pieces)]
    right = []
    for index, value in zip(indices, values):
        low = jnp.bitwise_and(index, lanes - 1).astype(jnp.float32)
        high = jnp.right_shift(index, 7)
        if halves:
            high = high + jnp.bitwise_and(jnp.right_shift(index, 6), 1) * rows
        high = high.astype(jnp.float32)
        parts = split(value, pieces)

        def wide(array, s, count):
            base = row_spread(array[s : s + 1, :], 16).astype(jnp.bfloat16)
            return jnp.concatenate([base] * (count // 16), axis=0)

        for s in range(SUB):
            right.append(jnp.where(lane_iota == wide(low, s, lanes), one, zero))
            hit = line_iota == wide(high, s, lines)
            for k in range(pieces):
                left[k].append(jnp.where(hit, wide(parts[k], s, lines), zero_lines))
    left = jnp.concatenate([jnp.concatenate(one_piece, axis=1) for one_piece in left], axis=0)
    right = jnp.concatenate(right, axis=1)
    both = lax.dot_general(left, right, (((1,), (1,)), ((), ())), preferred_element_type=jnp.float32)
    return both if halves else fold(both, rows, pieces)


def spread_table(field_ref, table, body, rows):
    for r in range(rows):
        table[body, r] = row_spread(field_ref[body, r : r + 1, :], SUB)


def stage(c, index, value, rows, staged):
    half = jnp.bitwise_and(jnp.right_shift(index, 6), 1) * rows
    staged[0, c] = jnp.bitwise_and(index, LANES // 2 - 1).astype(jnp.float32)
    staged[1, c] = (jnp.right_shift(index, 7) + half).astype(jnp.float32)
    head = value.astype(jnp.bfloat16).astype(jnp.float32)
    staged[2, c] = head
    staged[3, c] = value - head


def add_staged(rows, staged, sums, body):
    lanes = LANES // 2
    lines = 2 * rows
    lane_iota = lax.broadcasted_iota(jnp.int32, (lanes, LANES), 0).astype(jnp.float32).astype(jnp.bfloat16)
    line_iota = lax.broadcasted_iota(jnp.int32, (lines, LANES), 0).astype(jnp.float32).astype(jnp.bfloat16)
    one = jnp.ones((lanes, LANES), jnp.bfloat16)
    zero = jnp.zeros((lanes, LANES), jnp.bfloat16)
    zero_lines = jnp.zeros((lines, LANES), jnp.bfloat16)

    def wide(kind, c, s, count):
        base = row_spread(staged[kind, c, s : s + 1, :], 16).astype(jnp.bfloat16)
        return jnp.concatenate([base] * (count // 16), axis=0)

    left = [[], []]
    right = []
    for c in range(4):
        for s in range(SUB):
            right.append(jnp.where(lane_iota == wide(0, c, s, lanes), one, zero))
            hit = line_iota == wide(1, c, s, lines)
            for k in range(2):
                left[k].append(jnp.where(hit, wide(2 + k, c, s, lines), zero_lines))
    left = jnp.concatenate([jnp.concatenate(one_piece, axis=1) for one_piece in left], axis=0)
    right = jnp.concatenate(right, axis=1)
    sums[body] += lax.dot_general(
        left, right, (((1,), (1,)), ((), ())), preferred_element_type=jnp.float32
    )


def element_values(i, table, corners_ref, entries_ref, rows):
    chunks = entries_ref.shape[2] // SUB
    body = i // chunks
    j = lax.rem(i, chunks)
    first = pl.multiple_of(j * (4 * SUB), 4 * SUB)
    tile = pl.multiple_of(j * SUB, SUB)
    index = [corners_ref[body, pl.ds(first + c, SUB, stride=4), :] for c in range(4)]
    t = [pick(lambda r: table[body, r], rows, index[c]) for c in range(4)]
    k = [entries_ref[body, m, pl.ds(tile, SUB), :] for m in range(10)]
    out = [
        -(k[0] * t[0] + k[4] * t[1] + k[5] * t[2] + k[6] * t[3]),
        -(k[4] * t[0] + k[1] * t[1] + k[7] * t[2] + k[8] * t[3]),
        -(k[5] * t[0] + k[7] * t[1] + k[2] * t[2] + k[9] * t[3]),
        -(k[6] * t[0] + k[8] * t[1] + k[9] * t[2] + k[3] * t[3]),
    ]
    return index, out


def step_kernel(
    faces,
    layers,
    field_hbm,
    storage_hbm,
    corners_hbm,
    entries_hbm,
    rim_hbm,
    tri_hbm,
    match_hbm,
    flag_hbm,
    gap_hbm,
    motion_hbm,
    factor_hbm,
    out_ref,
    pressure_ref,
    field_ref,
    storage_ref,
    corners_ref,
    entries_ref,
    rim_ref,
    tri_ref,
    match_ref,
    flag_ref,
    gap_ref,
    motion_ref,
    factor_ref,
    load,
    disc_trace,
    rates,
    staged,
    table,
    sums,
    residual,
    pad,
    spread,
    landed,
    rim_out,
    rim_in,
    pad_send,
    pad_recv,
    rate_send,
    rate_recv,
    rim_send,
    rim_recv,
):
    rows = field_ref.shape[1]
    me = lax.axis_index("face")
    layer = lax.axis_index("depth")

    def fetch(k, source, target):
        copy = pltpu.make_async_copy(source, target, load.at[k])
        copy.start()
        return copy

    get_field = fetch(0, field_hbm, field_ref)
    get_tri = fetch(1, tri_hbm, tri_ref)
    get_motion = fetch(2, motion_hbm, motion_ref)
    get_corners = [fetch(3, corners_hbm.at[0], corners_ref.at[0])]
    get_entries = [fetch(4, entries_hbm.at[0], entries_ref.at[0])]
    get_corners.append(fetch(5, corners_hbm.at[1], corners_ref.at[1]))
    get_entries.append(fetch(6, entries_hbm.at[1], entries_ref.at[1]))
    get_rim = fetch(7, rim_hbm, rim_ref)
    get_rest = [
        fetch(8, match_hbm, match_ref),
        fetch(9, flag_hbm, flag_ref),
        fetch(10, gap_hbm, gap_ref),
        fetch(11, factor_hbm, factor_ref),
        fetch(12, storage_hbm, storage_ref),
    ]

    barrier = pltpu.get_barrier_semaphore()

    def greet(k, carry):
        peer = lax.rem(me + k, faces)
        pl.semaphore_signal(barrier, inc=1, device_id=(peer, layer), device_id_type=MESH)
        return carry

    lax.fori_loop(1, faces, greet, 0)

    @pl.when(layer > 0)
    def _():
        pl.semaphore_signal(barrier, inc=1, device_id=(me, layer - 1), device_id_type=MESH)

    @pl.when(layer < layers - 1)
    def _():
        pl.semaphore_signal(barrier, inc=1, device_id=(me, layer + 1), device_id_type=MESH)

    sums[...] = jnp.zeros_like(sums)
    staged[...] = jnp.zeros_like(staged)
    get_field.wait()
    get_tri.wait()
    get_motion.wait()
    for body in range(2):
        spread_table(field_ref, table, body, rows)
        t = [pick(lambda r: table[body, r], rows, tri_ref[body, c]) for c in range(3)]
        trace = (t[0] + t[1] + t[2]) / 3.0
        if body == 0:
            disc_trace[...] = trace
        else:
            pad[me, 1] = trace
    pad[me, 0] = motion_ref[...]
    around = (layer > 0).astype(jnp.int32) + (layer < layers - 1).astype(jnp.int32)
    line = lax.broadcasted_iota(jnp.int32, (SUB, LANES), 0)
    column = lax.broadcasted_iota(jnp.int32, (SUB, LANES), 1)
    zeros = jnp.zeros((SUB, LANES), jnp.float32)

    def pad_copy(slot, peer):
        return pltpu.make_async_remote_copy(
            src_ref=pad.at[slot],
            dst_ref=pad.at[slot],
            send_sem=pad_send.at[peer],
            recv_sem=pad_recv.at[slot],
            device_id=(peer, layer),
            device_id_type=MESH,
        )

    def send_pad(k, carry):
        pad_copy(me, lax.rem(me + k, faces)).start()
        return carry

    def wait_pad(k, carry):
        peer = lax.rem(me + k, faces)
        pad_copy(peer, peer).wait_recv()
        return carry

    def rate_copy(slot, peer):
        return pltpu.make_async_remote_copy(
            src_ref=spread.at[pl.ds(pl.multiple_of(peer * SUB, SUB), SUB)],
            dst_ref=landed.at[slot],
            send_sem=rate_send.at[peer],
            recv_sem=rate_recv.at[slot],
            device_id=(peer, layer),
            device_id_type=MESH,
        )

    def send_rate(k, carry):
        rate_copy(me, lax.rem(me + k, faces)).start()
        return carry

    def rate_faces():
        band = pl.multiple_of(me // SUB * SUB, SUB)
        mine = line == lax.rem(me, SUB)
        match = jnp.concatenate(
            [
                jnp.sum(
                    jnp.where(mine, match_ref[pl.ds(band, SUB), s * LANES : (s + 1) * LANES], 0),
                    axis=0,
                    keepdims=True,
                )
                for s in range(SUB)
            ],
            axis=0,
        )
        low = jnp.bitwise_and(match, LANES - 1)
        high = jnp.right_shift(match, 7)

        def look(patch, carry):
            normal, trace = carry
            for s in range(SUB):
                hit = high == patch * SUB + s
                for_normal = row_spread(pad[patch, 0, s : s + 1, :], SUB)
                for_trace = row_spread(pad[patch, 1, s : s + 1, :], SUB)
                normal = jnp.where(
                    hit, jnp.take_along_axis(for_normal, low, axis=1, mode="promise_in_bounds"), normal
                )
                trace = jnp.where(
                    hit, jnp.take_along_axis(for_trace, low, axis=1, mode="promise_in_bounds"), trace
                )
            return normal, trace

        normal, trace = lax.fori_loop(0, faces, look, (zeros, zeros))
        active = flag_ref[...].astype(jnp.float32)
        pressure = active * jnp.maximum(gap_ref[2] + nitsche * (gap_ref[0] - normal - gap_ref[1]), 0.0)
        pressure_ref[...] = pressure
        rate = active * factor_ref[...] * (film_floor + pressure) * (trace - disc_trace[...])
        rates[0] = rate
        spread[...] = add_into([match], [rate], faces * SUB, 3, halves=False)

    get_corners[0].wait()
    get_entries[0].wait()
    chunks = entries_ref.shape[2] // SUB
    steps = 2 * chunks

    def run(i, carry):
        @pl.when(i == steps // 8)
        def _():
            pl.semaphore_wait(barrier, faces - 1 + around)
            lax.fori_loop(1, faces, send_pad, 0)

        @pl.when(i == chunks)
        def _():
            get_corners[1].wait()
            get_entries[1].wait()

        @pl.when(i == steps * 5 // 8)
        def _():
            for one in get_rest:
                one.wait()
            lax.fori_loop(1, faces, wait_pad, 0)
            rate_faces()
            lax.fori_loop(1, faces, send_rate, 0)

        index, out = element_values(i, table, corners_ref, entries_ref, rows)
        add_staged(rows, staged, sums, jnp.maximum(i - 1, 0) // chunks)
        for c in range(4):
            stage(c, index[c], out[c], rows, staged)
        return carry

    lax.fori_loop(0, steps, run, 0)

    def wait_rate(k, total):
        peer = lax.rem(me + k, faces)
        rate_copy(peer, peer).wait_recv()
        return total + landed[peer]

    own = spread[pl.ds(pl.multiple_of(me * SUB, SUB), SUB), :]
    rates[1] = -lax.fori_loop(1, faces, wait_rate, own)
    surface = (layer == 0).astype(jnp.float32)

    def finish(k, carry):
        add_staged(rows, staged, sums, lax.rem(k + 1, 2))

        @pl.when(k < 2)
        def _():
            share = surface * rates[k] / 3.0
            for c in range(3):
                stage(c, tri_ref[k, c], share, rows, staged)
            stage(3, tri_ref[k, 0], zeros, rows, staged)

        return carry

    lax.fori_loop(0, 3, finish, 0)
    for body in range(2):
        residual[body] = join(sums[body], rows, 2)
    get_rim.wait()
    rim = rim_ref[...]

    at_rim = [
        pick(lambda r: row_spread(residual[body, r : r + 1, :], SUB), rows, rim) for body in range(2)
    ]
    rim_out[...] = jnp.where(line < SUB // 2, at_rim[0], at_rim[1])

    def rim_copy(slot, to):
        return pltpu.make_async_remote_copy(
            src_ref=rim_out,
            dst_ref=rim_in.at[slot],
            send_sem=rim_send.at[slot],
            recv_sem=rim_recv.at[slot],
            device_id=(me, to),
            device_id_type=MESH,
        )

    @pl.when(layer > 0)
    def _():
        rim_copy(1, layer - 1).start()

    @pl.when(layer < layers - 1)
    def _():
        rim_copy(0, layer + 1).start()

    @pl.when(layer == 0)
    def _():
        rim_in[0] = zeros

    @pl.when(layer == layers - 1)
    def _():
        rim_in[1] = zeros

    absent = SUB * LANES
    shift = jnp.where(line < SUB // 2, 0, rows * LANES)
    slot = line * LANES + column - absent
    where_rim = join(add_into([rim + shift], [slot.astype(jnp.float32)], 2 * rows, 2), 2 * rows, 2)
    where_rim = where_rim.astype(jnp.int32) + absent

    scale = [increment_factor / storage_ref[body] for body in range(2)]
    base = [field_ref[body] + residual[body] * scale[body] for body in range(2)]

    def drain(k, carry):
        peer = lax.rem(me + k, faces)
        pad_copy(me, peer).wait_send()
        rate_copy(me, peer).wait_send()
        return carry

    lax.fori_loop(1, faces, drain, 0)

    @pl.when(layer > 0)
    def _():
        rim_copy(0, layer - 1).wait_recv()

    @pl.when(layer < layers - 1)
    def _():
        rim_copy(1, layer + 1).wait_recv()

    from_below = jnp.concatenate([rim_in[0, 1:], rim_in[0, :1]], axis=0)
    from_above = jnp.concatenate([rim_in[1, SUB - 1 :], rim_in[1, : SUB - 1]], axis=0)
    more = jnp.where(jnp.bitwise_and(line, 1) == 0, from_below, from_above)
    more_rows = [row_spread(more[s : s + 1, :], SUB) for s in range(SUB)]
    for body in range(2):
        for part in range(rows // SUB):
            at = body * rows + part * SUB
            got = pick(lambda s: more_rows[s], SUB, where_rim[at : at + SUB])
            here = slice(part * SUB, (part + 1) * SUB)
            out_ref[body, here] = base[body][here] + scale[body][here] * got

    @pl.when(layer > 0)
    def _():
        rim_copy(1, layer - 1).wait_send()

    @pl.when(layer < layers - 1)
    def _():
        rim_copy(0, layer + 1).wait_send()


def local(
    faces,
    layers,
    thermal_field,
    lumped_storage,
    simplex_vertices,
    stiffness_entries,
    interface_vertices,
    touching_triangle_vertices,
    partner_lookup,
    engaged_flags,
    rotor_gap_quantities,
    lining_orthogonal_motion,
    touching_transfer_factor,
):
    nodes = thermal_field.shape[-1]
    rows = nodes // LANES
    tets = simplex_vertices.shape[-1]
    tiles = tets // LANES
    field = thermal_field.reshape(2, rows, LANES)
    storage = lumped_storage.reshape(2, rows, LANES)
    corners = (
        simplex_vertices.reshape(2, 4, tiles, LANES).transpose(0, 2, 1, 3).reshape(2, tiles * 4, LANES)
    )
    entries = stiffness_entries.reshape(2, 10, tiles, LANES)
    rim = (
        interface_vertices.reshape(2, 2, 2, LANES).transpose(0, 2, 1, 3).reshape(SUB, LANES)
    )
    tri = touching_triangle_vertices.reshape(2, 3, SUB, LANES)
    flags = engaged_flags.reshape(SUB, LANES)
    gaps = rotor_gap_quantities.reshape(3, SUB, LANES)
    motion = lining_orthogonal_motion.reshape(SUB, LANES)
    factor = touching_transfer_factor.reshape(SUB, LANES)
    vmem = pl.BlockSpec(memory_space=pltpu.VMEM)
    f32 = jnp.float32
    arrays = (field, storage, corners, entries, rim, tri, partner_lookup, flags, gaps, motion, factor)
    advanced, pressure = pl.pallas_call(
        functools.partial(step_kernel, faces, layers),
        out_shape=(
            pltpu.VMEM((2, rows, LANES), f32),
            pltpu.VMEM((SUB, LANES), f32),
        ),
        in_specs=[pl.BlockSpec(memory_space=pltpu.HBM)] * len(arrays),
        out_specs=(vmem, vmem),
        scratch_shapes=[pltpu.VMEM(array.shape, array.dtype) for array in arrays]
        + [
            pltpu.SemaphoreType.DMA((13,)),
            pltpu.VMEM((SUB, LANES), f32),
            pltpu.VMEM((2, SUB, LANES), f32),
            pltpu.VMEM((4, 4, SUB, LANES), f32),
            pltpu.VMEM((2, rows, SUB, LANES), f32),
            pltpu.VMEM((2, 4 * rows, LANES // 2), f32),
            pltpu.VMEM((2, rows, LANES), f32),
            pltpu.VMEM((faces, 2, SUB, LANES), f32),
            pltpu.VMEM((faces * SUB, LANES), f32),
            pltpu.VMEM((faces, SUB, LANES), f32),
            pltpu.VMEM((SUB, LANES), f32),
            pltpu.VMEM((2, SUB, LANES), f32),
            pltpu.SemaphoreType.DMA((faces,)),
            pltpu.SemaphoreType.DMA((faces,)),
            pltpu.SemaphoreType.DMA((faces,)),
            pltpu.SemaphoreType.DMA((faces,)),
            pltpu.SemaphoreType.DMA((2,)),
            pltpu.SemaphoreType.DMA((2,)),
        ],
        compiler_params=pltpu.CompilerParams(
            collective_id=0, has_side_effects=True, vmem_limit_bytes=60 * 1024 * 1024
        ),
        name="thermal_step",
    )(*arrays)
    return (advanced.reshape(thermal_field.shape), pressure.reshape(engaged_flags.shape))


def solution(mesh):
    placed = (
        P(None, "face", "depth", None),
        P(None, "face", "depth", None),
        P(None, "face", "depth", None, None),
        P(None, "face", "depth", None, None),
        P(None, "face", "depth", None, None),
        P(None, "face", None, None),
        P(),
        P("face", None),
        P(None, "face", None),
        P("face", None),
        P("face", None),
    )
    return jax.shard_map(
        functools.partial(local, mesh.shape["face"], mesh.shape["depth"]),
        mesh=mesh,
        in_specs=placed,
        out_specs=(P(None, "face", "depth", None), P("face", None)),
        check_vma=False,
    )
```

```python
import functools

import jax
import jax.numpy as jnp
from jax import lax
from jax.experimental import pallas as pl
from jax.experimental.pallas import tpu as pltpu
from jax.sharding import PartitionSpec as P

increment_factor = 0.05
nitsche = 1.0
film_floor = 0.25

LANES = 128
SUB = 8
MESH = pl.DeviceIdType.MESH


def row_spread(row, count):
    return jnp.broadcast_to(row, (count, LANES))


def pick(row_of, rows, index):
    low = jnp.bitwise_and(index, LANES - 1)
    high = jnp.right_shift(index, 7)
    out = jnp.zeros(index.shape, jnp.float32)
    for r in range(rows):
        got = jnp.take_along_axis(row_of(r), low, axis=1, mode="promise_in_bounds")
        out = jnp.where(high == r, got, out)
    return out


def split(value, pieces):
    parts = []
    for _ in range(pieces - 1):
        head = value.astype(jnp.bfloat16).astype(jnp.float32)
        parts.append(head)
        value = value - head
    parts.append(value)
    return parts


def fold(both, rows, pieces):
    total = both[:rows]
    for k in range(1, pieces):
        total = total + both[k * rows : (k + 1) * rows]
    return total


def join(both, rows, pieces):
    total = fold(both, 2 * rows, pieces)
    return jnp.concatenate([total[:rows], total[rows:]], axis=1)


def add_into(indices, values, rows, pieces, halves=True):
    lanes = LANES // 2 if halves else LANES
    lines = 2 * rows if halves else rows
    lane_iota = lax.broadcasted_iota(jnp.int32, (lanes, LANES), 0).astype(jnp.float32).astype(jnp.bfloat16)
    line_iota = lax.broadcasted_iota(jnp.int32, (lines, LANES), 0).astype(jnp.float32).astype(jnp.bfloat16)
    one = jnp.ones((lanes, LANES), jnp.bfloat16)
    zero = jnp.zeros((lanes, LANES), jnp.bfloat16)
    zero_lines = jnp.zeros((lines, LANES), jnp.bfloat16)
    left = [[] for _ in range(pieces)]
    right = []
    for index, value in zip(indices, values):
        low = jnp.bitwise_and(index, lanes - 1).astype(jnp.float32)
        high = jnp.right_shift(index, 7)
        if halves:
            high = high + jnp.bitwise_and(jnp.right_shift(index, 6), 1) * rows
        high = high.astype(jnp.float32)
        parts = split(value, pieces)

        def wide(array, s, count):
            base = row_spread(array[s : s + 1, :], 16).astype(jnp.bfloat16)
            return jnp.concatenate([base] * (count // 16), axis=0)

        for s in range(SUB):
            right.append(jnp.where(lane_iota == wide(low, s, lanes), one, zero))
            hit = line_iota == wide(high, s, lines)
            for k in range(pieces):
                left[k].append(jnp.where(hit, wide(parts[k], s, lines), zero_lines))
    left = jnp.concatenate([jnp.concatenate(one_piece, axis=1) for one_piece in left], axis=0)
    right = jnp.concatenate(right, axis=1)
    both = lax.dot_general(left, right, (((1,), (1,)), ((), ())), preferred_element_type=jnp.float32)
    return both if halves else fold(both, rows, pieces)


def spread_table(field_ref, table, body, rows):
    for r in range(rows):
        table[body, r] = row_spread(field_ref[body, r : r + 1, :], SUB)


def stage(c, index, value, rows, staged):
    half = jnp.bitwise_and(jnp.right_shift(index, 6), 1) * rows
    staged[0, c] = jnp.bitwise_and(index, LANES // 2 - 1).astype(jnp.float32)
    staged[1, c] = (jnp.right_shift(index, 7) + half).astype(jnp.float32)
    head = value.astype(jnp.bfloat16).astype(jnp.float32)
    staged[2, c] = head
    staged[3, c] = value - head


def add_staged(rows, staged, sums, body):
    lanes = LANES // 2
    lines = 2 * rows
    lane_iota = lax.broadcasted_iota(jnp.int32, (lanes, LANES), 0).astype(jnp.float32).astype(jnp.bfloat16)
    line_iota = lax.broadcasted_iota(jnp.int32, (lines, LANES), 0).astype(jnp.float32).astype(jnp.bfloat16)
    one = jnp.ones((lanes, LANES), jnp.bfloat16)
    zero = jnp.zeros((lanes, LANES), jnp.bfloat16)
    zero_lines = jnp.zeros((lines, LANES), jnp.bfloat16)

    def wide(kind, c, s, count):
        base = row_spread(staged[kind, c, s : s + 1, :], 16).astype(jnp.bfloat16)
        return jnp.concatenate([base] * (count // 16), axis=0)

    left = []
    right = []
    for c in range(4):
        blocks = [[], []]
        marks = []
        for s in range(SUB):
            marks.append(jnp.where(lane_iota == wide(0, c, s, lanes), one, zero))
            hit = line_iota == wide(1, c, s, lines)
            for k in range(2):
                blocks[k].append(jnp.where(hit, wide(2 + k, c, s, lines), zero_lines))
        left += [jnp.concatenate(block, axis=1) for block in blocks]
        right.append(jnp.concatenate(marks, axis=1))
    left = jnp.concatenate(left, axis=0)
    right = jnp.concatenate(right, axis=0)
    both = lax.dot_general(
        left, right, (((1,), (1,)), ((), ())), preferred_element_type=jnp.float32
    )
    side = 2 * lanes
    sums[body] += both[: 2 * 2 * lines, :side] + both[2 * 2 * lines :, side:]


def staged_total(total, rows):
    lanes = LANES // 2
    lines = 2 * rows
    return join(total[: 2 * lines, :lanes] + total[2 * lines :, lanes:], rows, 2)


def element_values(i, table, corners_ref, entries_ref, rows):
    chunks = entries_ref.shape[2] // SUB
    body = i // chunks
    j = lax.rem(i, chunks)
    first = pl.multiple_of(j * (4 * SUB), 4 * SUB)
    tile = pl.multiple_of(j * SUB, SUB)
    index = [corners_ref[body, pl.ds(first + c, SUB, stride=4), :] for c in range(4)]
    t = [pick(lambda r: table[body, r], rows, index[c]) for c in range(4)]
    k = [entries_ref[body, m, pl.ds(tile, SUB), :] for m in range(10)]
    out = [
        -(k[0] * t[0] + k[4] * t[1] + k[5] * t[2] + k[6] * t[3]),
        -(k[4] * t[0] + k[1] * t[1] + k[7] * t[2] + k[8] * t[3]),
        -(k[5] * t[0] + k[7] * t[1] + k[2] * t[2] + k[9] * t[3]),
        -(k[6] * t[0] + k[8] * t[1] + k[9] * t[2] + k[3] * t[3]),
    ]
    return index, out


def step_kernel(
    faces,
    layers,
    field_hbm,
    storage_hbm,
    corners_hbm,
    entries_hbm,
    rim_hbm,
    tri_hbm,
    match_hbm,
    flag_hbm,
    gap_hbm,
    motion_hbm,
    factor_hbm,
    out_ref,
    pressure_ref,
    field_ref,
    storage_ref,
    corners_ref,
    entries_ref,
    rim_ref,
    tri_ref,
    match_ref,
    flag_ref,
    gap_ref,
    motion_ref,
    factor_ref,
    load,
    disc_trace,
    rates,
    staged,
    table,
    sums,
    residual,
    pad,
    spread,
    landed,
    rim_out,
    rim_in,
    pad_send,
    pad_recv,
    rate_send,
    rate_recv,
    rim_send,
    rim_recv,
):
    rows = field_ref.shape[1]
    me = lax.axis_index("face")
    layer = lax.axis_index("depth")

    def fetch(k, source, target):
        copy = pltpu.make_async_copy(source, target, load.at[k])
        copy.start()
        return copy

    get_field = fetch(0, field_hbm, field_ref)
    get_tri = fetch(1, tri_hbm, tri_ref)
    get_motion = fetch(2, motion_hbm, motion_ref)
    get_corners = [fetch(3, corners_hbm.at[0], corners_ref.at[0])]
    get_entries = [fetch(4, entries_hbm.at[0], entries_ref.at[0])]
    get_corners.append(fetch(5, corners_hbm.at[1], corners_ref.at[1]))
    get_entries.append(fetch(6, entries_hbm.at[1], entries_ref.at[1]))
    get_rim = fetch(7, rim_hbm, rim_ref)
    get_rest = [
        fetch(8, match_hbm, match_ref),
        fetch(9, flag_hbm, flag_ref),
        fetch(10, gap_hbm, gap_ref),
        fetch(11, factor_hbm, factor_ref),
        fetch(12, storage_hbm, storage_ref),
    ]

    barrier = pltpu.get_barrier_semaphore()

    def greet(k, carry):
        peer = lax.rem(me + k, faces)
        pl.semaphore_signal(barrier, inc=1, device_id=(peer, layer), device_id_type=MESH)
        return carry

    lax.fori_loop(1, faces, greet, 0)

    @pl.when(layer > 0)
    def _():
        pl.semaphore_signal(barrier, inc=1, device_id=(me, layer - 1), device_id_type=MESH)

    @pl.when(layer < layers - 1)
    def _():
        pl.semaphore_signal(barrier, inc=1, device_id=(me, layer + 1), device_id_type=MESH)

    sums[...] = jnp.zeros_like(sums)
    staged[...] = jnp.zeros_like(staged)
    get_field.wait()
    get_tri.wait()
    get_motion.wait()
    for body in range(2):
        spread_table(field_ref, table, body, rows)
        t = [pick(lambda r: table[body, r], rows, tri_ref[body, c]) for c in range(3)]
        trace = (t[0] + t[1] + t[2]) / 3.0
        if body == 0:
            disc_trace[...] = trace
        else:
            pad[me, 1] = trace
    pad[me, 0] = motion_ref[...]
    around = (layer > 0).astype(jnp.int32) + (layer < layers - 1).astype(jnp.int32)
    line = lax.broadcasted_iota(jnp.int32, (SUB, LANES), 0)
    column = lax.broadcasted_iota(jnp.int32, (SUB, LANES), 1)
    zeros = jnp.zeros((SUB, LANES), jnp.float32)

    def pad_copy(slot, peer):
        return pltpu.make_async_remote_copy(
            src_ref=pad.at[slot],
            dst_ref=pad.at[slot],
            send_sem=pad_send.at[peer],
            recv_sem=pad_recv.at[slot],
            device_id=(peer, layer),
            device_id_type=MESH,
        )

    def send_pad(k, carry):
        pad_copy(me, lax.rem(me + k, faces)).start()
        return carry

    def wait_pad(k, carry):
        peer = lax.rem(me + k, faces)
        pad_copy(peer, peer).wait_recv()
        return carry

    def rate_copy(slot, peer):
        return pltpu.make_async_remote_copy(
            src_ref=spread.at[pl.ds(pl.multiple_of(peer * SUB, SUB), SUB)],
            dst_ref=landed.at[slot],
            send_sem=rate_send.at[peer],
            recv_sem=rate_recv.at[slot],
            device_id=(peer, layer),
            device_id_type=MESH,
        )

    def send_rate(k, carry):
        rate_copy(me, lax.rem(me + k, faces)).start()
        return carry

    def rate_faces():
        band = pl.multiple_of(me // SUB * SUB, SUB)
        mine = line == lax.rem(me, SUB)
        match = jnp.concatenate(
            [
                jnp.sum(
                    jnp.where(mine, match_ref[pl.ds(band, SUB), s * LANES : (s + 1) * LANES], 0),
                    axis=0,
                    keepdims=True,
                )
                for s in range(SUB)
            ],
            axis=0,
        )
        low = jnp.bitwise_and(match, LANES - 1)
        high = jnp.right_shift(match, 7)

        def look(turn, carry):
            normal, trace = carry
            for at in range(4 * SUB):
                patch = turn * 4 + at // SUB
                s = at % SUB
                hit = high == patch * SUB + s
                for_normal = row_spread(pad[patch, 0, s : s + 1, :], SUB)
                for_trace = row_spread(pad[patch, 1, s : s + 1, :], SUB)
                normal = jnp.where(
                    hit, jnp.take_along_axis(for_normal, low, axis=1, mode="promise_in_bounds"), normal
                )
                trace = jnp.where(
                    hit, jnp.take_along_axis(for_trace, low, axis=1, mode="promise_in_bounds"), trace
                )
            return normal, trace

        normal, trace = lax.fori_loop(0, faces // 4, look, (zeros, zeros))
        active = flag_ref[...].astype(jnp.float32)
        pressure = active * jnp.maximum(gap_ref[2] + nitsche * (gap_ref[0] - normal - gap_ref[1]), 0.0)
        pressure_ref[...] = pressure
        rate = active * factor_ref[...] * (film_floor + pressure) * (trace - disc_trace[...])
        rates[0] = rate
        spread[...] = add_into([match], [rate], faces * SUB, 3, halves=False)

    get_corners[0].wait()
    get_entries[0].wait()
    chunks = entries_ref.shape[2] // SUB
    steps = 2 * chunks

    def run(i, carry):
        @pl.when(i == steps // 8)
        def _():
            pl.semaphore_wait(barrier, faces - 1 + around)
            for k in range(1, faces):
                send_pad(k, 0)

        @pl.when(i == chunks)
        def _():
            get_corners[1].wait()
            get_entries[1].wait()

        @pl.when(i == steps * 5 // 8)
        def _():
            for one in get_rest:
                one.wait()
            lax.fori_loop(1, faces, wait_pad, 0)
            rate_faces()
            for k in range(1, faces):
                send_rate(k, 0)

        index, out = element_values(i, table, corners_ref, entries_ref, rows)
        add_staged(rows, staged, sums, jnp.maximum(i - 1, 0) // chunks)
        for c in range(4):
            stage(c, index[c], out[c], rows, staged)
        return carry

    lax.fori_loop(0, steps, run, 0)

    def wait_rate(k, total):
        peer = lax.rem(me + k, faces)
        rate_copy(peer, peer).wait_recv()
        return total + landed[peer]

    own = spread[pl.ds(pl.multiple_of(me * SUB, SUB), SUB), :]
    rates[1] = -lax.fori_loop(1, faces, wait_rate, own)
    surface = (layer == 0).astype(jnp.float32)

    def finish(k, carry):
        add_staged(rows, staged, sums, lax.rem(k + 1, 2))

        @pl.when(k < 2)
        def _():
            share = surface * rates[k] / 3.0
            for c in range(3):
                stage(c, tri_ref[k, c], share, rows, staged)
            stage(3, tri_ref[k, 0], zeros, rows, staged)

        return carry

    lax.fori_loop(0, 3, finish, 0)
    for body in range(2):
        residual[body] = staged_total(sums[body], rows)
    get_rim.wait()
    rim = rim_ref[...]

    at_rim = [
        pick(lambda r: row_spread(residual[body, r : r + 1, :], SUB), rows, rim) for body in range(2)
    ]
    rim_out[...] = jnp.where(line < SUB // 2, at_rim[0], at_rim[1])

    def rim_copy(slot, to):
        return pltpu.make_async_remote_copy(
            src_ref=rim_out,
            dst_ref=rim_in.at[slot],
            send_sem=rim_send.at[slot],
            recv_sem=rim_recv.at[slot],
            device_id=(me, to),
            device_id_type=MESH,
        )

    @pl.when(layer > 0)
    def _():
        rim_copy(1, layer - 1).start()

    @pl.when(layer < layers - 1)
    def _():
        rim_copy(0, layer + 1).start()

    @pl.when(layer == 0)
    def _():
        rim_in[0] = zeros

    @pl.when(layer == layers - 1)
    def _():
        rim_in[1] = zeros

    absent = SUB * LANES
    shift = jnp.where(line < SUB // 2, 0, rows * LANES)
    slot = line * LANES + column - absent
    where_rim = join(add_into([rim + shift], [slot.astype(jnp.float32)], 2 * rows, 2), 2 * rows, 2)
    where_rim = where_rim.astype(jnp.int32) + absent

    scale = [increment_factor / storage_ref[body] for body in range(2)]
    base = [field_ref[body] + residual[body] * scale[body] for body in range(2)]

    def drain(k, carry):
        peer = lax.rem(me + k, faces)
        pad_copy(me, peer).wait_send()
        rate_copy(me, peer).wait_send()
        return carry

    lax.fori_loop(1, faces, drain, 0)

    @pl.when(layer > 0)
    def _():
        rim_copy(0, layer - 1).wait_recv()

    @pl.when(layer < layers - 1)
    def _():
        rim_copy(1, layer + 1).wait_recv()

    from_below = jnp.concatenate([rim_in[0, 1:], rim_in[0, :1]], axis=0)
    from_above = jnp.concatenate([rim_in[1, SUB - 1 :], rim_in[1, : SUB - 1]], axis=0)
    more = jnp.where(jnp.bitwise_and(line, 1) == 0, from_below, from_above)
    more_rows = [row_spread(more[s : s + 1, :], SUB) for s in range(SUB)]
    for body in range(2):
        for part in range(rows // SUB):
            at = body * rows + part * SUB
            got = pick(lambda s: more_rows[s], SUB, where_rim[at : at + SUB])
            here = slice(part * SUB, (part + 1) * SUB)
            out_ref[body, here] = base[body][here] + scale[body][here] * got

    @pl.when(layer > 0)
    def _():
        rim_copy(1, layer - 1).wait_send()

    @pl.when(layer < layers - 1)
    def _():
        rim_copy(0, layer + 1).wait_send()


def local(
    faces,
    layers,
    thermal_field,
    lumped_storage,
    simplex_vertices,
    stiffness_entries,
    interface_vertices,
    touching_triangle_vertices,
    partner_lookup,
    engaged_flags,
    rotor_gap_quantities,
    lining_orthogonal_motion,
    touching_transfer_factor,
):
    nodes = thermal_field.shape[-1]
    rows = nodes // LANES
    tets = simplex_vertices.shape[-1]
    tiles = tets // LANES
    field = thermal_field.reshape(2, rows, LANES)
    storage = lumped_storage.reshape(2, rows, LANES)
    corners = (
        simplex_vertices.reshape(2, 4, tiles, LANES).transpose(0, 2, 1, 3).reshape(2, tiles * 4, LANES)
    )
    entries = stiffness_entries.reshape(2, 10, tiles, LANES)
    rim = (
        interface_vertices.reshape(2, 2, 2, LANES).transpose(0, 2, 1, 3).reshape(SUB, LANES)
    )
    tri = touching_triangle_vertices.reshape(2, 3, SUB, LANES)
    flags = engaged_flags.reshape(SUB, LANES)
    gaps = rotor_gap_quantities.reshape(3, SUB, LANES)
    motion = lining_orthogonal_motion.reshape(SUB, LANES)
    factor = touching_transfer_factor.reshape(SUB, LANES)
    vmem = pl.BlockSpec(memory_space=pltpu.VMEM)
    f32 = jnp.float32
    arrays = (field, storage, corners, entries, rim, tri, partner_lookup, flags, gaps, motion, factor)
    advanced, pressure = pl.pallas_call(
        functools.partial(step_kernel, faces, layers),
        out_shape=(
            pltpu.VMEM((2, rows, LANES), f32),
            pltpu.VMEM((SUB, LANES), f32),
        ),
        in_specs=[pl.BlockSpec(memory_space=pltpu.HBM)] * len(arrays),
        out_specs=(vmem, vmem),
        scratch_shapes=[pltpu.VMEM(array.shape, array.dtype) for array in arrays]
        + [
            pltpu.SemaphoreType.DMA((13,)),
            pltpu.VMEM((SUB, LANES), f32),
            pltpu.VMEM((2, SUB, LANES), f32),
            pltpu.VMEM((4, 4, SUB, LANES), f32),
            pltpu.VMEM((2, rows, SUB, LANES), f32),
            pltpu.VMEM((2, 8 * rows, LANES), f32),
            pltpu.VMEM((2, rows, LANES), f32),
            pltpu.VMEM((faces, 2, SUB, LANES), f32),
            pltpu.VMEM((faces * SUB, LANES), f32),
            pltpu.VMEM((faces, SUB, LANES), f32),
            pltpu.VMEM((SUB, LANES), f32),
            pltpu.VMEM((2, SUB, LANES), f32),
            pltpu.SemaphoreType.DMA((faces,)),
            pltpu.SemaphoreType.DMA((faces,)),
            pltpu.SemaphoreType.DMA((faces,)),
            pltpu.SemaphoreType.DMA((faces,)),
            pltpu.SemaphoreType.DMA((2,)),
            pltpu.SemaphoreType.DMA((2,)),
        ],
        compiler_params=pltpu.CompilerParams(
            collective_id=0, has_side_effects=True, vmem_limit_bytes=60 * 1024 * 1024
        ),
        name="thermal_step",
    )(*arrays)
    return (advanced.reshape(thermal_field.shape), pressure.reshape(engaged_flags.shape))


def solution(mesh):
    placed = (
        P(None, "face", "depth", None),
        P(None, "face", "depth", None),
        P(None, "face", "depth", None, None),
        P(None, "face", "depth", None, None),
        P(None, "face", "depth", None, None),
        P(None, "face", None, None),
        P(),
        P("face", None),
        P(None, "face", None),
        P("face", None),
        P("face", None),
    )
    return jax.shard_map(
        functools.partial(local, mesh.shape["face"], mesh.shape["depth"]),
        mesh=mesh,
        in_specs=placed,
        out_specs=(P(None, "face", "depth", None), P("face", None)),
        check_vma=False,
    )
```

```python
import functools

import jax
import jax.numpy as jnp
from jax import lax
from jax.experimental import pallas as pl
from jax.experimental.pallas import tpu as pltpu
from jax.sharding import PartitionSpec as P

increment_factor = 0.05
nitsche = 1.0
film_floor = 0.25

LANES = 128
SUB = 8
MESH = pl.DeviceIdType.MESH
GROUP = 2


def row_spread(row, count):
    return jnp.broadcast_to(row, (count, LANES))


def pick(row_of, rows, index):
    low = jnp.bitwise_and(index, LANES - 1)
    high = jnp.right_shift(index, 7)
    out = jnp.zeros(index.shape, jnp.float32)
    for r in range(rows):
        got = jnp.take_along_axis(row_of(r), low, axis=1, mode="promise_in_bounds")
        out = jnp.where(high == r, got, out)
    return out


def split(value, pieces):
    parts = []
    for _ in range(pieces - 1):
        head = value.astype(jnp.bfloat16).astype(jnp.float32)
        parts.append(head)
        value = value - head
    parts.append(value)
    return parts


def fold(both, rows, pieces):
    total = both[:rows]
    for k in range(1, pieces):
        total = total + both[k * rows : (k + 1) * rows]
    return total


def join(both, rows, pieces):
    total = fold(both, 2 * rows, pieces)
    return jnp.concatenate([total[:rows], total[rows:]], axis=1)


def add_into(indices, values, rows, pieces, halves=True):
    lanes = LANES // 2 if halves else LANES
    lines = 2 * rows if halves else rows
    lane_iota = lax.broadcasted_iota(jnp.int32, (lanes, LANES), 0).astype(jnp.float32).astype(jnp.bfloat16)
    line_iota = lax.broadcasted_iota(jnp.int32, (lines, LANES), 0).astype(jnp.float32).astype(jnp.bfloat16)
    one = jnp.ones((lanes, LANES), jnp.bfloat16)
    zero = jnp.zeros((lanes, LANES), jnp.bfloat16)
    zero_lines = jnp.zeros((lines, LANES), jnp.bfloat16)
    left = [[] for _ in range(pieces)]
    right = []
    for index, value in zip(indices, values):
        low = jnp.bitwise_and(index, lanes - 1).astype(jnp.float32)
        high = jnp.right_shift(index, 7)
        if halves:
            high = high + jnp.bitwise_and(jnp.right_shift(index, 6), 1) * rows
        high = high.astype(jnp.float32)
        parts = split(value, pieces)

        def wide(array, s, count):
            base = row_spread(array[s : s + 1, :], 16).astype(jnp.bfloat16)
            return jnp.concatenate([base] * (count // 16), axis=0)

        for s in range(SUB):
            right.append(jnp.where(lane_iota == wide(low, s, lanes), one, zero))
            hit = line_iota == wide(high, s, lines)
            for k in range(pieces):
                left[k].append(jnp.where(hit, wide(parts[k], s, lines), zero_lines))
    left = jnp.concatenate([jnp.concatenate(one_piece, axis=1) for one_piece in left], axis=0)
    right = jnp.concatenate(right, axis=1)
    both = lax.dot_general(left, right, (((1,), (1,)), ((), ())), preferred_element_type=jnp.float32)
    return both if halves else fold(both, rows, pieces)


def spread_table(field_ref, table, body, rows):
    for r in range(rows):
        table[body, r] = row_spread(field_ref[body, r : r + 1, :], SUB)


def stage(c, u, index, value, rows, staged):
    here = slice(u * SUB, (u + 1) * SUB)
    half = jnp.bitwise_and(jnp.right_shift(index, 6), 1) * rows
    staged[0, c, here] = jnp.bitwise_and(index, LANES // 2 - 1).astype(jnp.float32)
    staged[1, c, here] = (jnp.right_shift(index, 7) + half).astype(jnp.float32)
    head = value.astype(jnp.bfloat16).astype(jnp.float32)
    staged[2, c, here] = head
    staged[3, c, here] = value - head


def add_staged(rows, staged, sums, body):
    lanes = LANES // 2
    lines = 2 * rows
    lane_iota = lax.broadcasted_iota(jnp.int32, (lanes, LANES), 0).astype(jnp.float32).astype(jnp.bfloat16)
    line_iota = lax.broadcasted_iota(jnp.int32, (lines, LANES), 0).astype(jnp.float32).astype(jnp.bfloat16)
    one = jnp.ones((lanes, LANES), jnp.bfloat16)
    zero = jnp.zeros((lanes, LANES), jnp.bfloat16)
    zero_lines = jnp.zeros((lines, LANES), jnp.bfloat16)

    def wide(kind, c, s, count):
        base = row_spread(staged[kind, c, s : s + 1, :], 16).astype(jnp.bfloat16)
        return jnp.concatenate([base] * (count // 16), axis=0)

    left = []
    right = []
    for c in range(4):
        blocks = [[], []]
        marks = []
        for s in range(GROUP * SUB):
            marks.append(jnp.where(lane_iota == wide(0, c, s, lanes), one, zero))
            hit = line_iota == wide(1, c, s, lines)
            for k in range(2):
                blocks[k].append(jnp.where(hit, wide(2 + k, c, s, lines), zero_lines))
        left += [jnp.concatenate(block, axis=1) for block in blocks]
        right.append(jnp.concatenate(marks, axis=1))
    left = jnp.concatenate(left, axis=0)
    right = jnp.concatenate(right, axis=0)
    both = lax.dot_general(
        left, right, (((1,), (1,)), ((), ())), preferred_element_type=jnp.float32
    )
    side = 2 * lanes
    sums[body] += both[: 2 * 2 * lines, :side] + both[2 * 2 * lines :, side:]


def staged_total(total, rows):
    lanes = LANES // 2
    lines = 2 * rows
    return join(total[: 2 * lines, :lanes] + total[2 * lines :, lanes:], rows, 2)


def element_values(body, j, table, corners_ref, entries_ref, rows):
    first = pl.multiple_of(j * (4 * SUB), 4 * SUB)
    tile = pl.multiple_of(j * SUB, SUB)
    index = [corners_ref[body, pl.ds(first + c, SUB, stride=4), :] for c in range(4)]
    t = [pick(lambda r: table[body, r], rows, index[c]) for c in range(4)]
    k = [entries_ref[body, m, pl.ds(tile, SUB), :] for m in range(10)]
    out = [
        -(k[0] * t[0] + k[4] * t[1] + k[5] * t[2] + k[6] * t[3]),
        -(k[4] * t[0] + k[1] * t[1] + k[7] * t[2] + k[8] * t[3]),
        -(k[5] * t[0] + k[7] * t[1] + k[2] * t[2] + k[9] * t[3]),
        -(k[6] * t[0] + k[8] * t[1] + k[9] * t[2] + k[3] * t[3]),
    ]
    return index, out


def step_kernel(
    faces,
    layers,
    field_hbm,
    storage_hbm,
    corners_hbm,
    entries_hbm,
    rim_hbm,
    tri_hbm,
    match_hbm,
    flag_hbm,
    gap_hbm,
    motion_hbm,
    factor_hbm,
    out_ref,
    pressure_ref,
    field_ref,
    storage_ref,
    corners_ref,
    entries_ref,
    rim_ref,
    tri_ref,
    match_ref,
    flag_ref,
    gap_ref,
    motion_ref,
    factor_ref,
    load,
    disc_trace,
    rates,
    staged,
    table,
    sums,
    residual,
    pad,
    spread,
    landed,
    rim_out,
    rim_in,
    pad_send,
    pad_recv,
    rate_send,
    rate_recv,
    rim_send,
    rim_recv,
):
    rows = field_ref.shape[1]
    me = lax.axis_index("face")
    layer = lax.axis_index("depth")

    def fetch(k, source, target):
        copy = pltpu.make_async_copy(source, target, load.at[k])
        copy.start()
        return copy

    get_field = fetch(0, field_hbm, field_ref)
    get_tri = fetch(1, tri_hbm, tri_ref)
    get_motion = fetch(2, motion_hbm, motion_ref)
    get_corners = [fetch(3, corners_hbm.at[0], corners_ref.at[0])]
    get_entries = [fetch(4, entries_hbm.at[0], entries_ref.at[0])]
    get_corners.append(fetch(5, corners_hbm.at[1], corners_ref.at[1]))
    get_entries.append(fetch(6, entries_hbm.at[1], entries_ref.at[1]))
    get_rim = fetch(7, rim_hbm, rim_ref)
    get_rest = [
        fetch(8, match_hbm, match_ref),
        fetch(9, flag_hbm, flag_ref),
        fetch(10, gap_hbm, gap_ref),
        fetch(11, factor_hbm, factor_ref),
        fetch(12, storage_hbm, storage_ref),
    ]

    barrier = pltpu.get_barrier_semaphore()

    def greet(k, carry):
        peer = lax.rem(me + k, faces)
        pl.semaphore_signal(barrier, inc=1, device_id=(peer, layer), device_id_type=MESH)
        return carry

    lax.fori_loop(1, faces, greet, 0)

    @pl.when(layer > 0)
    def _():
        pl.semaphore_signal(barrier, inc=1, device_id=(me, layer - 1), device_id_type=MESH)

    @pl.when(layer < layers - 1)
    def _():
        pl.semaphore_signal(barrier, inc=1, device_id=(me, layer + 1), device_id_type=MESH)

    sums[...] = jnp.zeros_like(sums)
    staged[...] = jnp.zeros_like(staged)
    get_field.wait()
    get_tri.wait()
    get_motion.wait()
    for body in range(2):
        spread_table(field_ref, table, body, rows)
        t = [pick(lambda r: table[body, r], rows, tri_ref[body, c]) for c in range(3)]
        trace = (t[0] + t[1] + t[2]) / 3.0
        if body == 0:
            disc_trace[...] = trace
        else:
            pad[me, 1] = trace
    pad[me, 0] = motion_ref[...]
    around = (layer > 0).astype(jnp.int32) + (layer < layers - 1).astype(jnp.int32)
    line = lax.broadcasted_iota(jnp.int32, (SUB, LANES), 0)
    column = lax.broadcasted_iota(jnp.int32, (SUB, LANES), 1)
    zeros = jnp.zeros((SUB, LANES), jnp.float32)

    def pad_copy(slot, peer):
        return pltpu.make_async_remote_copy(
            src_ref=pad.at[slot],
            dst_ref=pad.at[slot],
            send_sem=pad_send.at[peer],
            recv_sem=pad_recv.at[slot],
            device_id=(peer, layer),
            device_id_type=MESH,
        )

    def send_pad(k, carry):
        pad_copy(me, lax.rem(me + k, faces)).start()
        return carry

    def wait_pad(k, carry):
        peer = lax.rem(me + k, faces)
        pad_copy(peer, peer).wait_recv()
        return carry

    def rate_copy(slot, peer):
        return pltpu.make_async_remote_copy(
            src_ref=spread.at[pl.ds(pl.multiple_of(peer * SUB, SUB), SUB)],
            dst_ref=landed.at[slot],
            send_sem=rate_send.at[peer],
            recv_sem=rate_recv.at[slot],
            device_id=(peer, layer),
            device_id_type=MESH,
        )

    def send_rate(k, carry):
        rate_copy(me, lax.rem(me + k, faces)).start()
        return carry

    def rate_faces():
        band = pl.multiple_of(me // SUB * SUB, SUB)
        mine = line == lax.rem(me, SUB)
        match = jnp.concatenate(
            [
                jnp.sum(
                    jnp.where(mine, match_ref[pl.ds(band, SUB), s * LANES : (s + 1) * LANES], 0),
                    axis=0,
                    keepdims=True,
                )
                for s in range(SUB)
            ],
            axis=0,
        )
        low = jnp.bitwise_and(match, LANES - 1)
        high = jnp.right_shift(match, 7)

        def look(turn, carry):
            normal, trace = carry
            for at in range(4 * SUB):
                patch = turn * 4 + at // SUB
                s = at % SUB
                hit = high == patch * SUB + s
                for_normal = row_spread(pad[patch, 0, s : s + 1, :], SUB)
                for_trace = row_spread(pad[patch, 1, s : s + 1, :], SUB)
                normal = jnp.where(
                    hit, jnp.take_along_axis(for_normal, low, axis=1, mode="promise_in_bounds"), normal
                )
                trace = jnp.where(
                    hit, jnp.take_along_axis(for_trace, low, axis=1, mode="promise_in_bounds"), trace
                )
            return normal, trace

        normal, trace = lax.fori_loop(0, faces // 4, look, (zeros, zeros))
        active = flag_ref[...].astype(jnp.float32)
        pressure = active * jnp.maximum(gap_ref[2] + nitsche * (gap_ref[0] - normal - gap_ref[1]), 0.0)
        pressure_ref[...] = pressure
        rate = active * factor_ref[...] * (film_floor + pressure) * (trace - disc_trace[...])
        rates[0] = rate
        spread[...] = add_into([match], [rate], faces * SUB, 3, halves=False)

    get_corners[0].wait()
    get_entries[0].wait()
    turns = entries_ref.shape[2] // (GROUP * SUB)
    steps = 2 * turns

    def run(i, carry):
        @pl.when(i == steps // 8)
        def _():
            pl.semaphore_wait(barrier, faces - 1 + around)
            for k in range(1, faces):
                send_pad(k, 0)

        @pl.when(i == turns)
        def _():
            get_corners[1].wait()
            get_entries[1].wait()

        @pl.when(i == steps * 5 // 8)
        def _():
            for one in get_rest:
                one.wait()
            lax.fori_loop(1, faces, wait_pad, 0)
            rate_faces()
            for k in range(1, faces):
                send_rate(k, 0)

        made = [
            element_values(
                i // turns, lax.rem(i, turns) * GROUP + u, table, corners_ref, entries_ref, rows
            )
            for u in range(GROUP)
        ]
        add_staged(rows, staged, sums, jnp.maximum(i - 1, 0) // turns)
        for u, (index, out) in enumerate(made):
            for c in range(4):
                stage(c, u, index[c], out[c], rows, staged)
        return carry

    lax.fori_loop(0, steps, run, 0)

    def wait_rate(k, total):
        peer = lax.rem(me + k, faces)
        rate_copy(peer, peer).wait_recv()
        return total + landed[peer]

    own = spread[pl.ds(pl.multiple_of(me * SUB, SUB), SUB), :]
    rates[1] = -lax.fori_loop(1, faces, wait_rate, own)
    surface = (layer == 0).astype(jnp.float32)

    add_staged(rows, staged, sums, 1)
    at_faces = []
    shares = []
    for body in range(2):
        share = surface * rates[body] / 3.0
        at_faces += [tri_ref[body, c] + body * rows * LANES for c in range(3)]
        shares += [share] * 3
    contact = join(add_into(at_faces, shares, 2 * rows, 2), 2 * rows, 2)
    for body in range(2):
        residual[body] = staged_total(sums[body], rows) + contact[body * rows : (body + 1) * rows]
    get_rim.wait()
    rim = rim_ref[...]

    at_rim = [
        pick(lambda r: row_spread(residual[body, r : r + 1, :], SUB), rows, rim) for body in range(2)
    ]
    rim_out[...] = jnp.where(line < SUB // 2, at_rim[0], at_rim[1])

    def rim_copy(slot, to):
        return pltpu.make_async_remote_copy(
            src_ref=rim_out,
            dst_ref=rim_in.at[slot],
            send_sem=rim_send.at[slot],
            recv_sem=rim_recv.at[slot],
            device_id=(me, to),
            device_id_type=MESH,
        )

    @pl.when(layer > 0)
    def _():
        rim_copy(1, layer - 1).start()

    @pl.when(layer < layers - 1)
    def _():
        rim_copy(0, layer + 1).start()

    @pl.when(layer == 0)
    def _():
        rim_in[0] = zeros

    @pl.when(layer == layers - 1)
    def _():
        rim_in[1] = zeros

    absent = SUB * LANES
    shift = jnp.where(line < SUB // 2, 0, rows * LANES)
    slot = line * LANES + column - absent
    where_rim = join(add_into([rim + shift], [slot.astype(jnp.float32)], 2 * rows, 2), 2 * rows, 2)
    where_rim = where_rim.astype(jnp.int32) + absent

    scale = [increment_factor / storage_ref[body] for body in range(2)]
    base = [field_ref[body] + residual[body] * scale[body] for body in range(2)]

    def drain(k, carry):
        peer = lax.rem(me + k, faces)
        pad_copy(me, peer).wait_send()
        rate_copy(me, peer).wait_send()
        return carry

    lax.fori_loop(1, faces, drain, 0)

    @pl.when(layer > 0)
    def _():
        rim_copy(0, layer - 1).wait_recv()

    @pl.when(layer < layers - 1)
    def _():
        rim_copy(1, layer + 1).wait_recv()

    from_below = jnp.concatenate([rim_in[0, 1:], rim_in[0, :1]], axis=0)
    from_above = jnp.concatenate([rim_in[1, SUB - 1 :], rim_in[1, : SUB - 1]], axis=0)
    more = jnp.where(jnp.bitwise_and(line, 1) == 0, from_below, from_above)
    more_rows = [row_spread(more[s : s + 1, :], SUB) for s in range(SUB)]
    for body in range(2):
        for part in range(rows // SUB):
            at = body * rows + part * SUB
            got = pick(lambda s: more_rows[s], SUB, where_rim[at : at + SUB])
            here = slice(part * SUB, (part + 1) * SUB)
            out_ref[body, here] = base[body][here] + scale[body][here] * got

    @pl.when(layer > 0)
    def _():
        rim_copy(1, layer - 1).wait_send()

    @pl.when(layer < layers - 1)
    def _():
        rim_copy(0, layer + 1).wait_send()


def local(
    faces,
    layers,
    thermal_field,
    lumped_storage,
    simplex_vertices,
    stiffness_entries,
    interface_vertices,
    touching_triangle_vertices,
    partner_lookup,
    engaged_flags,
    rotor_gap_quantities,
    lining_orthogonal_motion,
    touching_transfer_factor,
):
    nodes = thermal_field.shape[-1]
    rows = nodes // LANES
    tets = simplex_vertices.shape[-1]
    tiles = tets // LANES
    field = thermal_field.reshape(2, rows, LANES)
    storage = lumped_storage.reshape(2, rows, LANES)
    corners = (
        simplex_vertices.reshape(2, 4, tiles, LANES).transpose(0, 2, 1, 3).reshape(2, tiles * 4, LANES)
    )
    entries = stiffness_entries.reshape(2, 10, tiles, LANES)
    rim = (
        interface_vertices.reshape(2, 2, 2, LANES).transpose(0, 2, 1, 3).reshape(SUB, LANES)
    )
    tri = touching_triangle_vertices.reshape(2, 3, SUB, LANES)
    flags = engaged_flags.reshape(SUB, LANES)
    gaps = rotor_gap_quantities.reshape(3, SUB, LANES)
    motion = lining_orthogonal_motion.reshape(SUB, LANES)
    factor = touching_transfer_factor.reshape(SUB, LANES)
    vmem = pl.BlockSpec(memory_space=pltpu.VMEM)
    f32 = jnp.float32
    arrays = (field, storage, corners, entries, rim, tri, partner_lookup, flags, gaps, motion, factor)
    advanced, pressure = pl.pallas_call(
        functools.partial(step_kernel, faces, layers),
        out_shape=(
            pltpu.VMEM((2, rows, LANES), f32),
            pltpu.VMEM((SUB, LANES), f32),
        ),
        in_specs=[pl.BlockSpec(memory_space=pltpu.HBM)] * len(arrays),
        out_specs=(vmem, vmem),
        scratch_shapes=[pltpu.VMEM(array.shape, array.dtype) for array in arrays]
        + [
            pltpu.SemaphoreType.DMA((13,)),
            pltpu.VMEM((SUB, LANES), f32),
            pltpu.VMEM((2, SUB, LANES), f32),
            pltpu.VMEM((4, 4, GROUP * SUB, LANES), f32),
            pltpu.VMEM((2, rows, SUB, LANES), f32),
            pltpu.VMEM((2, 8 * rows, LANES), f32),
            pltpu.VMEM((2, rows, LANES), f32),
            pltpu.VMEM((faces, 2, SUB, LANES), f32),
            pltpu.VMEM((faces * SUB, LANES), f32),
            pltpu.VMEM((faces, SUB, LANES), f32),
            pltpu.VMEM((SUB, LANES), f32),
            pltpu.VMEM((2, SUB, LANES), f32),
            pltpu.SemaphoreType.DMA((faces,)),
            pltpu.SemaphoreType.DMA((faces,)),
            pltpu.SemaphoreType.DMA((faces,)),
            pltpu.SemaphoreType.DMA((faces,)),
            pltpu.SemaphoreType.DMA((2,)),
            pltpu.SemaphoreType.DMA((2,)),
        ],
        compiler_params=pltpu.CompilerParams(
            collective_id=0, has_side_effects=True, vmem_limit_bytes=60 * 1024 * 1024
        ),
        name="thermal_step",
    )(*arrays)
    return (advanced.reshape(thermal_field.shape), pressure.reshape(engaged_flags.shape))


def solution(mesh):
    placed = (
        P(None, "face", "depth", None),
        P(None, "face", "depth", None),
        P(None, "face", "depth", None, None),
        P(None, "face", "depth", None, None),
        P(None, "face", "depth", None, None),
        P(None, "face", None, None),
        P(),
        P("face", None),
        P(None, "face", None),
        P("face", None),
        P("face", None),
    )
    return jax.shard_map(
        functools.partial(local, mesh.shape["face"], mesh.shape["depth"]),
        mesh=mesh,
        in_specs=placed,
        out_specs=(P(None, "face", "depth", None), P("face", None)),
        check_vma=False,
    )
```

```python
import functools

import jax
import jax.numpy as jnp
from jax import lax
from jax.experimental import pallas as pl
from jax.experimental.pallas import tpu as pltpu
from jax.sharding import PartitionSpec as P

increment_factor = 0.05
nitsche = 1.0
film_floor = 0.25

LANES = 128
SUB = 8
MESH = pl.DeviceIdType.MESH
GROUP = 2


def row_spread(row, count):
    return jnp.broadcast_to(row, (count, LANES))


def pick(row_of, rows, index):
    low = jnp.bitwise_and(index, LANES - 1)
    high = jnp.right_shift(index, 7)
    out = jnp.zeros(index.shape, jnp.float32)
    for r in range(rows):
        got = jnp.take_along_axis(row_of(r), low, axis=1, mode="promise_in_bounds")
        out = jnp.where(high == r, got, out)
    return out


def split(value, pieces):
    parts = []
    for _ in range(pieces - 1):
        head = value.astype(jnp.bfloat16).astype(jnp.float32)
        parts.append(head)
        value = value - head
    parts.append(value)
    return parts


def fold(both, rows, pieces):
    total = both[:rows]
    for k in range(1, pieces):
        total = total + both[k * rows : (k + 1) * rows]
    return total


def join(both, rows, pieces):
    total = fold(both, 2 * rows, pieces)
    return jnp.concatenate([total[:rows], total[rows:]], axis=1)


def add_into(indices, values, rows, pieces, halves=True):
    lanes = LANES // 2 if halves else LANES
    lines = 2 * rows if halves else rows
    lane_iota = lax.broadcasted_iota(jnp.int32, (lanes, LANES), 0).astype(jnp.float32).astype(jnp.bfloat16)
    line_iota = lax.broadcasted_iota(jnp.int32, (lines, LANES), 0).astype(jnp.float32).astype(jnp.bfloat16)
    one = jnp.ones((lanes, LANES), jnp.bfloat16)
    zero = jnp.zeros((lanes, LANES), jnp.bfloat16)
    zero_lines = jnp.zeros((lines, LANES), jnp.bfloat16)
    left = [[] for _ in range(pieces)]
    right = []
    for index, value in zip(indices, values):
        low = jnp.bitwise_and(index, lanes - 1).astype(jnp.float32)
        high = jnp.right_shift(index, 7)
        if halves:
            high = high + jnp.bitwise_and(jnp.right_shift(index, 6), 1) * rows
        high = high.astype(jnp.float32)
        parts = split(value, pieces)

        def wide(array, s, count):
            base = row_spread(array[s : s + 1, :], 16).astype(jnp.bfloat16)
            return jnp.concatenate([base] * (count // 16), axis=0)

        for s in range(SUB):
            right.append(jnp.where(lane_iota == wide(low, s, lanes), one, zero))
            hit = line_iota == wide(high, s, lines)
            for k in range(pieces):
                left[k].append(jnp.where(hit, wide(parts[k], s, lines), zero_lines))
    left = jnp.concatenate([jnp.concatenate(one_piece, axis=1) for one_piece in left], axis=0)
    right = jnp.concatenate(right, axis=1)
    both = lax.dot_general(left, right, (((1,), (1,)), ((), ())), preferred_element_type=jnp.float32)
    return both if halves else fold(both, rows, pieces)


def spread_table(field_ref, table, body, rows):
    for r in range(rows):
        table[body, r] = row_spread(field_ref[body, r : r + 1, :], SUB)


def stage(c, u, index, value, rows, staged):
    here = slice(u * SUB, (u + 1) * SUB)
    half = jnp.bitwise_and(jnp.right_shift(index, 6), 1) * rows
    staged[0, c, here] = jnp.bitwise_and(index, LANES // 2 - 1).astype(jnp.float32)
    staged[1, c, here] = (jnp.right_shift(index, 7) + half).astype(jnp.float32)
    head = value.astype(jnp.bfloat16).astype(jnp.float32)
    staged[2, c, here] = head
    staged[3, c, here] = value - head


def add_staged(rows, staged, sums, body):
    lanes = LANES // 2
    lines = 2 * rows
    lane_iota = lax.broadcasted_iota(jnp.int32, (lanes, LANES), 0).astype(jnp.float32).astype(jnp.bfloat16)
    line_iota = lax.broadcasted_iota(jnp.int32, (lines, LANES), 0).astype(jnp.float32).astype(jnp.bfloat16)
    one = jnp.ones((lanes, LANES), jnp.bfloat16)
    zero = jnp.zeros((lanes, LANES), jnp.bfloat16)
    zero_lines = jnp.zeros((lines, LANES), jnp.bfloat16)

    def wide(kind, c, s, count):
        base = row_spread(staged[kind, c, s : s + 1, :], 16).astype(jnp.bfloat16)
        return jnp.concatenate([base] * (count // 16), axis=0)

    left = []
    right = []
    for c in range(4):
        blocks = [[], []]
        marks = []
        for s in range(GROUP * SUB):
            marks.append(jnp.where(lane_iota == wide(0, c, s, lanes), one, zero))
            hit = line_iota == wide(1, c, s, lines)
            for k in range(2):
                blocks[k].append(jnp.where(hit, wide(2 + k, c, s, lines), zero_lines))
        left += [jnp.concatenate(block, axis=1) for block in blocks]
        right.append(jnp.concatenate(marks, axis=1))
    left = jnp.concatenate(left, axis=0)
    right = jnp.concatenate(right, axis=0)
    both = lax.dot_general(
        left, right, (((1,), (1,)), ((), ())), preferred_element_type=jnp.float32
    )
    side = 2 * lanes
    sums[body] += both[: 2 * 2 * lines, :side] + both[2 * 2 * lines :, side:]


def staged_total(total, rows):
    lanes = LANES // 2
    lines = 2 * rows
    return join(total[: 2 * lines, :lanes] + total[2 * lines :, lanes:], rows, 2)


def element_values(body, j, table, corners_ref, entries_ref, rows):
    first = pl.multiple_of(j * (4 * SUB), 4 * SUB)
    tile = pl.multiple_of(j * SUB, SUB)
    index = [corners_ref[body, pl.ds(first + c, SUB, stride=4), :] for c in range(4)]
    t = [pick(lambda r: table[body, r], rows, index[c]) for c in range(4)]
    k = [entries_ref[body, m, pl.ds(tile, SUB), :] for m in range(10)]
    out = [
        -(k[0] * t[0] + k[4] * t[1] + k[5] * t[2] + k[6] * t[3]),
        -(k[4] * t[0] + k[1] * t[1] + k[7] * t[2] + k[8] * t[3]),
        -(k[5] * t[0] + k[7] * t[1] + k[2] * t[2] + k[9] * t[3]),
        -(k[6] * t[0] + k[8] * t[1] + k[9] * t[2] + k[3] * t[3]),
    ]
    return index, out


def step_kernel(
    faces,
    layers,
    field_hbm,
    storage_hbm,
    corners_hbm,
    entries_hbm,
    rim_hbm,
    tri_hbm,
    match_hbm,
    flag_hbm,
    gap_hbm,
    motion_hbm,
    factor_hbm,
    out_ref,
    pressure_ref,
    field_ref,
    storage_ref,
    corners_ref,
    entries_ref,
    rim_ref,
    tri_ref,
    match_ref,
    flag_ref,
    gap_ref,
    motion_ref,
    factor_ref,
    load,
    disc_trace,
    rates,
    staged,
    table,
    sums,
    residual,
    pad,
    spread,
    landed,
    rim_out,
    rim_in,
    pad_send,
    pad_recv,
    rate_send,
    rate_recv,
    rim_send,
    rim_recv,
):
    rows = field_ref.shape[1]
    me = lax.axis_index("face")
    layer = lax.axis_index("depth")

    def fetch(k, source, target):
        copy = pltpu.make_async_copy(source, target, load.at[k])
        copy.start()
        return copy

    get_field = fetch(0, field_hbm, field_ref)
    get_tri = fetch(1, tri_hbm, tri_ref)
    get_motion = fetch(2, motion_hbm, motion_ref)
    get_corners = [fetch(3, corners_hbm.at[0], corners_ref.at[0])]
    get_entries = [fetch(4, entries_hbm.at[0], entries_ref.at[0])]
    get_corners.append(fetch(5, corners_hbm.at[1], corners_ref.at[1]))
    get_entries.append(fetch(6, entries_hbm.at[1], entries_ref.at[1]))
    get_rim = fetch(7, rim_hbm, rim_ref)
    get_rest = [
        fetch(8, match_hbm, match_ref),
        fetch(9, flag_hbm, flag_ref),
        fetch(10, gap_hbm, gap_ref),
        fetch(11, factor_hbm, factor_ref),
        fetch(12, storage_hbm, storage_ref),
    ]

    barrier = pltpu.get_barrier_semaphore()

    def greet(k, carry):
        peer = lax.rem(me + k, faces)
        pl.semaphore_signal(barrier, inc=1, device_id=(peer, layer), device_id_type=MESH)
        return carry

    lax.fori_loop(1, faces, greet, 0)

    @pl.when(layer > 0)
    def _():
        pl.semaphore_signal(barrier, inc=1, device_id=(me, layer - 1), device_id_type=MESH)

    @pl.when(layer < layers - 1)
    def _():
        pl.semaphore_signal(barrier, inc=1, device_id=(me, layer + 1), device_id_type=MESH)

    sums[...] = jnp.zeros_like(sums)
    staged[...] = jnp.zeros_like(staged)
    get_field.wait()
    get_tri.wait()
    get_motion.wait()
    for body in range(2):
        spread_table(field_ref, table, body, rows)
        t = [pick(lambda r: table[body, r], rows, tri_ref[body, c]) for c in range(3)]
        trace = (t[0] + t[1] + t[2]) / 3.0
        if body == 0:
            disc_trace[...] = trace
        else:
            pad[me, 1] = trace
    pad[me, 0] = motion_ref[...]
    around = (layer > 0).astype(jnp.int32) + (layer < layers - 1).astype(jnp.int32)
    line = lax.broadcasted_iota(jnp.int32, (SUB, LANES), 0)
    column = lax.broadcasted_iota(jnp.int32, (SUB, LANES), 1)
    zeros = jnp.zeros((SUB, LANES), jnp.float32)

    def pad_copy(slot, peer):
        return pltpu.make_async_remote_copy(
            src_ref=pad.at[slot],
            dst_ref=pad.at[slot],
            send_sem=pad_send.at[peer],
            recv_sem=pad_recv.at[slot],
            device_id=(peer, layer),
            device_id_type=MESH,
        )

    def send_pad(k, carry):
        pad_copy(me, lax.rem(me + k, faces)).start()
        return carry

    def wait_pad(k, carry):
        peer = lax.rem(me + k, faces)
        pad_copy(peer, peer).wait_recv()
        return carry

    def rate_copy(slot, peer):
        return pltpu.make_async_remote_copy(
            src_ref=spread.at[pl.ds(pl.multiple_of(peer * SUB, SUB), SUB)],
            dst_ref=landed.at[slot],
            send_sem=rate_send.at[peer],
            recv_sem=rate_recv.at[slot],
            device_id=(peer, layer),
            device_id_type=MESH,
        )

    def send_rate(k, carry):
        rate_copy(me, lax.rem(me + k, faces)).start()
        return carry

    def rate_faces():
        band = pl.multiple_of(me // SUB * SUB, SUB)
        mine = line == lax.rem(me, SUB)
        match = jnp.concatenate(
            [
                jnp.sum(
                    jnp.where(mine, match_ref[pl.ds(band, SUB), s * LANES : (s + 1) * LANES], 0),
                    axis=0,
                    keepdims=True,
                )
                for s in range(SUB)
            ],
            axis=0,
        )
        low = jnp.bitwise_and(match, LANES - 1)
        high = jnp.right_shift(match, 7)

        def look(turn, carry):
            normal, trace = carry
            for at in range(4 * SUB):
                patch = turn * 4 + at // SUB
                s = at % SUB
                hit = high == patch * SUB + s
                for_normal = row_spread(pad[patch, 0, s : s + 1, :], SUB)
                for_trace = row_spread(pad[patch, 1, s : s + 1, :], SUB)
                normal = jnp.where(
                    hit, jnp.take_along_axis(for_normal, low, axis=1, mode="promise_in_bounds"), normal
                )
                trace = jnp.where(
                    hit, jnp.take_along_axis(for_trace, low, axis=1, mode="promise_in_bounds"), trace
                )
            return normal, trace

        normal, trace = lax.fori_loop(0, faces // 4, look, (zeros, zeros))
        active = flag_ref[...].astype(jnp.float32)
        pressure = active * jnp.maximum(gap_ref[2] + nitsche * (gap_ref[0] - normal - gap_ref[1]), 0.0)
        pressure_ref[...] = pressure
        rate = active * factor_ref[...] * (film_floor + pressure) * (trace - disc_trace[...])
        rates[0] = rate
        spread[...] = add_into([match], [rate], faces * SUB, 3, halves=False)

    get_corners[0].wait()
    get_entries[0].wait()
    turns = entries_ref.shape[2] // (GROUP * SUB)
    steps = 2 * turns

    def run(i, carry):
        @pl.when(i == 0)
        def _():
            pl.semaphore_wait(barrier, faces - 1 + around)
            for k in range(1, faces):
                send_pad(k, 0)

        @pl.when(i == turns)
        def _():
            get_corners[1].wait()
            get_entries[1].wait()

        @pl.when(i == steps * 3 // 8)
        def _():
            for one in get_rest:
                one.wait()
            lax.fori_loop(1, faces, wait_pad, 0)
            rate_faces()
            for k in range(1, faces):
                send_rate(k, 0)

        made = [
            element_values(
                i // turns, lax.rem(i, turns) * GROUP + u, table, corners_ref, entries_ref, rows
            )
            for u in range(GROUP)
        ]
        add_staged(rows, staged, sums, jnp.maximum(i - 1, 0) // turns)
        for u, (index, out) in enumerate(made):
            for c in range(4):
                stage(c, u, index[c], out[c], rows, staged)
        return carry

    lax.fori_loop(0, steps, run, 0)

    def wait_rate(k, total):
        peer = lax.rem(me + k, faces)
        rate_copy(peer, peer).wait_recv()
        return total + landed[peer]

    own = spread[pl.ds(pl.multiple_of(me * SUB, SUB), SUB), :]
    rates[1] = -lax.fori_loop(1, faces, wait_rate, own)
    surface = (layer == 0).astype(jnp.float32)

    add_staged(rows, staged, sums, 1)
    at_faces = []
    shares = []
    for body in range(2):
        share = surface * rates[body] / 3.0
        at_faces += [tri_ref[body, c] + body * rows * LANES for c in range(3)]
        shares += [share] * 3
    contact = join(add_into(at_faces, shares, 2 * rows, 2), 2 * rows, 2)
    for body in range(2):
        residual[body] = staged_total(sums[body], rows) + contact[body * rows : (body + 1) * rows]
    get_rim.wait()
    rim = rim_ref[...]

    at_rim = [
        pick(lambda r: row_spread(residual[body, r : r + 1, :], SUB), rows, rim) for body in range(2)
    ]
    rim_out[...] = jnp.where(line < SUB // 2, at_rim[0], at_rim[1])

    def rim_copy(slot, to):
        return pltpu.make_async_remote_copy(
            src_ref=rim_out,
            dst_ref=rim_in.at[slot],
            send_sem=rim_send.at[slot],
            recv_sem=rim_recv.at[slot],
            device_id=(me, to),
            device_id_type=MESH,
        )

    @pl.when(layer > 0)
    def _():
        rim_copy(1, layer - 1).start()

    @pl.when(layer < layers - 1)
    def _():
        rim_copy(0, layer + 1).start()

    @pl.when(layer == 0)
    def _():
        rim_in[0] = zeros

    @pl.when(layer == layers - 1)
    def _():
        rim_in[1] = zeros

    absent = SUB * LANES
    shift = jnp.where(line < SUB // 2, 0, rows * LANES)
    slot = line * LANES + column - absent
    where_rim = join(add_into([rim + shift], [slot.astype(jnp.float32)], 2 * rows, 2), 2 * rows, 2)
    where_rim = where_rim.astype(jnp.int32) + absent

    scale = [increment_factor / storage_ref[body] for body in range(2)]
    base = [field_ref[body] + residual[body] * scale[body] for body in range(2)]

    def drain(k, carry):
        peer = lax.rem(me + k, faces)
        pad_copy(me, peer).wait_send()
        rate_copy(me, peer).wait_send()
        return carry

    lax.fori_loop(1, faces, drain, 0)

    @pl.when(layer > 0)
    def _():
        rim_copy(0, layer - 1).wait_recv()

    @pl.when(layer < layers - 1)
    def _():
        rim_copy(1, layer + 1).wait_recv()

    from_below = jnp.concatenate([rim_in[0, 1:], rim_in[0, :1]], axis=0)
    from_above = jnp.concatenate([rim_in[1, SUB - 1 :], rim_in[1, : SUB - 1]], axis=0)
    more = jnp.where(jnp.bitwise_and(line, 1) == 0, from_below, from_above)
    more_rows = [row_spread(more[s : s + 1, :], SUB) for s in range(SUB)]
    for body in range(2):
        for part in range(rows // SUB):
            at = body * rows + part * SUB
            got = pick(lambda s: more_rows[s], SUB, where_rim[at : at + SUB])
            here = slice(part * SUB, (part + 1) * SUB)
            out_ref[body, here] = base[body][here] + scale[body][here] * got

    @pl.when(layer > 0)
    def _():
        rim_copy(1, layer - 1).wait_send()

    @pl.when(layer < layers - 1)
    def _():
        rim_copy(0, layer + 1).wait_send()


def local(
    faces,
    layers,
    thermal_field,
    lumped_storage,
    simplex_vertices,
    stiffness_entries,
    interface_vertices,
    touching_triangle_vertices,
    partner_lookup,
    engaged_flags,
    rotor_gap_quantities,
    lining_orthogonal_motion,
    touching_transfer_factor,
):
    nodes = thermal_field.shape[-1]
    rows = nodes // LANES
    tets = simplex_vertices.shape[-1]
    tiles = tets // LANES
    field = thermal_field.reshape(2, rows, LANES)
    storage = lumped_storage.reshape(2, rows, LANES)
    corners = (
        simplex_vertices.reshape(2, 4, tiles, LANES).transpose(0, 2, 1, 3).reshape(2, tiles * 4, LANES)
    )
    entries = stiffness_entries.reshape(2, 10, tiles, LANES)
    rim = (
        interface_vertices.reshape(2, 2, 2, LANES).transpose(0, 2, 1, 3).reshape(SUB, LANES)
    )
    tri = touching_triangle_vertices.reshape(2, 3, SUB, LANES)
    flags = engaged_flags.reshape(SUB, LANES)
    gaps = rotor_gap_quantities.reshape(3, SUB, LANES)
    motion = lining_orthogonal_motion.reshape(SUB, LANES)
    factor = touching_transfer_factor.reshape(SUB, LANES)
    vmem = pl.BlockSpec(memory_space=pltpu.VMEM)
    f32 = jnp.float32
    arrays = (field, storage, corners, entries, rim, tri, partner_lookup, flags, gaps, motion, factor)
    advanced, pressure = pl.pallas_call(
        functools.partial(step_kernel, faces, layers),
        out_shape=(
            pltpu.VMEM((2, rows, LANES), f32),
            pltpu.VMEM((SUB, LANES), f32),
        ),
        in_specs=[pl.BlockSpec(memory_space=pltpu.HBM)] * len(arrays),
        out_specs=(vmem, vmem),
        scratch_shapes=[pltpu.VMEM(array.shape, array.dtype) for array in arrays]
        + [
            pltpu.SemaphoreType.DMA((13,)),
            pltpu.VMEM((SUB, LANES), f32),
            pltpu.VMEM((2, SUB, LANES), f32),
            pltpu.VMEM((4, 4, GROUP * SUB, LANES), f32),
            pltpu.VMEM((2, rows, SUB, LANES), f32),
            pltpu.VMEM((2, 8 * rows, LANES), f32),
            pltpu.VMEM((2, rows, LANES), f32),
            pltpu.VMEM((faces, 2, SUB, LANES), f32),
            pltpu.VMEM((faces * SUB, LANES), f32),
            pltpu.VMEM((faces, SUB, LANES), f32),
            pltpu.VMEM((SUB, LANES), f32),
            pltpu.VMEM((2, SUB, LANES), f32),
            pltpu.SemaphoreType.DMA((faces,)),
            pltpu.SemaphoreType.DMA((faces,)),
            pltpu.SemaphoreType.DMA((faces,)),
            pltpu.SemaphoreType.DMA((faces,)),
            pltpu.SemaphoreType.DMA((2,)),
            pltpu.SemaphoreType.DMA((2,)),
        ],
        compiler_params=pltpu.CompilerParams(
            collective_id=0, has_side_effects=True, vmem_limit_bytes=60 * 1024 * 1024
        ),
        name="thermal_step",
    )(*arrays)
    return (advanced.reshape(thermal_field.shape), pressure.reshape(engaged_flags.shape))


def solution(mesh):
    placed = (
        P(None, "face", "depth", None),
        P(None, "face", "depth", None),
        P(None, "face", "depth", None, None),
        P(None, "face", "depth", None, None),
        P(None, "face", "depth", None, None),
        P(None, "face", None, None),
        P(),
        P("face", None),
        P(None, "face", None),
        P("face", None),
        P("face", None),
    )
    return jax.shard_map(
        functools.partial(local, mesh.shape["face"], mesh.shape["depth"]),
        mesh=mesh,
        in_specs=placed,
        out_specs=(P(None, "face", "depth", None), P("face", None)),
        check_vma=False,
    )
```
